128 devices in a mesh: pipe: 4 (over z), expert: 32 (over x, y, core).
Axes of the slice: x: 4, y: 4, z: 4, core: 2. Of those that a mesh axis runs over, the one named last changes fastest.
Arguments:
- expert_inputs: bfloat16 [4, 1, 32, 32, 5, 4096], P('pipe', None, 'expert'), may hold values from -6 to 6
- routes: int32 [4, 1, 4096, 1], P('pipe', None, 'expert'), may hold values from 0 to 15; in each aligned block of 128 rows (0 to 127, 128 to 255, ..., all dimensions but the last counted through in order) at most 10 rows name the same one
- gate_prob: float32 [4, 1, 4096, 1], P('pipe', None, 'expert'), may hold values from 0.25 to 1
- out_grad: bfloat16 [1, 4096, 4096], P(None, 'expert'), may hold values from -6 to 6
- gate_weight: bfloat16 [4, 4096, 12288], P('pipe', None, 'expert'), may hold values from -0.09375 to 0.09375
- up_weight: bfloat16 [4, 4096, 12288], P('pipe', None, 'expert'), may hold values from -0.09375 to 0.09375
- down_weight: bfloat16 [4, 12288, 4096], P('pipe', 'expert'), may hold values from -0.21875 to 0.21875
Outputs:
- input_grads: bfloat16 [4, 1, 4096, 4096], P('pipe', None, 'expert')
- gate_grad: bfloat16 [4, 4096, 12288], P('pipe', None, 'expert')
- up_grad: bfloat16 [4, 4096, 12288], P('pipe', None, 'expert')
- down_grad: bfloat16 [4, 12288, 4096], P('pipe', 'expert')
The draws below stay inside these ranges and needn't reach their ends.
Inputs may be any that keep to these rules, and one draw needn't show every extreme that they name: `routes`: in every section and micro-batch the 128 tokens of one block name each expert at most 10 times, and some block names one expert exactly 10 times.
All inputs are finite; a program needn't handle non-finite values.
Results may differ from the reference program's by a relative error of at most 0.015.
Values may be sent and summed in bfloat16 or wider, within the bound.
A program may use at most 128 MiB of HBM per device.

```python
import math
import jax
import jax.numpy as jnp
import numpy as np
from jax import lax

D = 4096
HID = 768
TOP = 1
MB = 1
TOK_DEV = 128
EXPERTS = 16
HID_DEV = 384
TOKENS = 4096
CAP = 10
HALF = 5
N_PIPE = 4
N_EXPERT = 32


def block_scale(rng, dims, cuts, least, largest):
    factor_of = 1.0
    for axis_at, shards_of in cuts:
        draws = jax.random.uniform(jax.random.fold_in(jax.random.fold_in(rng, 6), axis_at), (shards_of,), jnp.float32, least / len(cuts), largest / len(cuts))
        factor_of = factor_of * jnp.repeat(jnp.exp(draws), dims[axis_at] // shards_of).reshape((-1,) + (1,) * (len(dims) - 1 - axis_at))
    return factor_of


def shared_out(key, own, number, rows, count, top, most, skew):
    order = jax.random.permutation(key, count)
    packed, ordinary = portions_of(count, rows * top, most, skew, True), portions_of(count, rows * top, most, skew, False)
    places = jnp.arange(count)

    def named(lengths, rotation):
        used = int((lengths > 0).sum())
        fixed = max(1, used // 4)
        shifted = fixed + (places - fixed + rotation * (used - fixed)) % max(1, count - fixed)
        return jnp.zeros((count,), jnp.int32).at[order[jnp.where(places < fixed, places, shifted)]].set(jnp.asarray(lengths, jnp.int32))

    lengths = jnp.where(number % 4 == 0, named(packed, number // 4), named(ordinary, number - number // 4 - 1))
    mixed = jax.random.permutation(jax.random.fold_in(own, 3), count)
    source_of, sink = mixed[0:count // 2 * 2:2], mixed[1:count // 2 * 2:2]
    slack = jnp.minimum(lengths[source_of] - 1, most - lengths[sink]) // 2
    slack = jnp.where((source_of == order[0]) | (sink == order[0]) | (lengths[sink] == 0), 0, jnp.maximum(slack, 0))
    shifted = jax.random.randint(jax.random.fold_in(own, 4), (count // 2,), 0, 1 << 20) % (slack + 1)
    lengths = lengths.at[source_of].add(-shifted).at[sink].add(shifted)
    labels = jnp.searchsorted(jnp.cumsum(lengths), jnp.arange(rows * top), side="right").astype(jnp.int32)
    listing = labels.reshape(top, rows).T
    listing = listing[jax.random.permutation(jax.random.fold_in(own, 1), rows)]
    rotation = jax.random.randint(jax.random.fold_in(own, 2), (rows, 1), 0, top)
    return jnp.take_along_axis(listing, (jnp.arange(top)[None, :] + rotation) % top, axis=1)


def portions_of(count, total, reach, skew, full):
    portions = [(1 << 20) // math.isqrt(grade ** skew) + 1 for grade in range(1, count + 1)]
    largest = reach if full else min(reach, max(-(-total // count), total * portions[0] // sum(portions)))
    least = 1 if total - largest >= count - 1 else 0
    counts, spare = [largest] + [least] * (count - 1), total - largest - least * (count - 1)
    while spare > 0:
        candidates = [i for i in range(1, count) if counts[i] < largest] or [i for i in range(1, count) if counts[i] < reach]
        pool, budget = sum([portions[i] for i in candidates]), spare
        for i in candidates:
            addition = min(reach - counts[i], max(1, budget * portions[i] // pool), spare)
            counts[i] = counts[i] + addition
            spare = spare - addition
    return np.array(counts)


def gaussian(stream_key, extent, spread, limit, pieces=(), held_as=jnp.bfloat16):
    factor_of = block_scale(stream_key, extent, pieces, -0.22, 0.18) if pieces else 1.0
    entries = jax.random.normal(stream_key, extent, jnp.float32) * spread * factor_of
    return jnp.minimum(jnp.maximum(entries, -limit), limit).astype(held_as)


def setup_inputs(seed: int = 0) -> dict:
    key_of = jax.random.split(jax.random.key(seed), 8)
    expert_inputs = gaussian(key_of[0], (N_PIPE, MB, N_EXPERT, N_EXPERT, HALF, D), 1.0, 6.0, ((0, 4), (2, 32)))
    routes_keys = jax.random.split(jax.random.fold_in(key_of[1], 1), N_PIPE * MB * TOKENS // TOK_DEV)
    routes_turns = jax.random.permutation(jax.random.fold_in(key_of[1], 3), N_PIPE * MB * TOKENS // TOK_DEV)
    routes = jax.vmap(lambda own, number: shared_out(jax.random.fold_in(key_of[1], 2), own, number, TOK_DEV, EXPERTS, TOP, CAP, 2))(routes_keys, routes_turns).reshape((N_PIPE, MB, TOKENS, TOP))
    gate_prob = jnp.clip(0.25 + 0.75 * jax.random.uniform(key_of[2], (N_PIPE, MB, TOKENS, TOP), jnp.float32) ** block_scale(key_of[2], (N_PIPE, MB, TOKENS, TOP), ((0, 4), (2, 32)), -0.2, 0.2), 0.25, 1.0)
    out_grad = gaussian(key_of[3], (MB, TOKENS, D), 1.0, 6.0, ((1, 32),))
    gate_weight = gaussian(key_of[4], (N_PIPE, D, EXPERTS * HID), D ** -0.5, 0.09375, ((0, 4), (2, 32)))
    up_weight = gaussian(key_of[5], (N_PIPE, D, EXPERTS * HID), D ** -0.5, 0.09375, ((0, 4), (2, 32)))
    down_weight = gaussian(key_of[6], (N_PIPE, EXPERTS * HID, D), HID ** -0.5, 0.21875, ((0, 4), (1, 32)))
    return dict(expert_inputs=expert_inputs, routes=routes, gate_prob=gate_prob, out_grad=out_grad, gate_weight=gate_weight, up_weight=up_weight, down_weight=down_weight)


def half_backward(inputs, rows, w_gate, w_up, w_down):
    pre_gate = jnp.dot(inputs, w_gate, preferred_element_type=jnp.float32)
    pre_up = jnp.dot(inputs, w_up, preferred_element_type=jnp.float32)
    sigmoid_gate = jax.nn.sigmoid(pre_gate)
    silu_gate = pre_gate * sigmoid_gate
    hidden = (silu_gate * pre_up).astype(jnp.bfloat16)
    delta_hidden = jnp.dot(rows, w_down.T, preferred_element_type=jnp.float32)
    delta_up = (delta_hidden * silu_gate).astype(jnp.bfloat16)
    delta_gate = (delta_hidden * pre_up * sigmoid_gate * (1.0 + pre_gate * (1.0 - sigmoid_gate))).astype(jnp.bfloat16)
    partial_sum = (jnp.dot(delta_gate, w_gate.T, preferred_element_type=jnp.float32)
                   + jnp.dot(delta_up, w_up.T, preferred_element_type=jnp.float32)).astype(jnp.bfloat16)
    grad_gate = jnp.dot(inputs.T, delta_gate, preferred_element_type=jnp.float32)
    grad_up = jnp.dot(inputs.T, delta_up, preferred_element_type=jnp.float32)
    grad_down = jnp.dot(hidden.T, rows, preferred_element_type=jnp.float32)
    return partial_sum, grad_gate, grad_up, grad_down


def per_expert(items):
    rows, inputs, gate_cols, up_cols, down_rows = items
    first = half_backward(inputs, rows, gate_cols[0], up_cols[0], down_rows[0])
    second = half_backward(inputs, rows, gate_cols[1], up_cols[1], down_rows[1])
    back = (first[0].astype(jnp.float32) + second[0].astype(jnp.float32)).astype(jnp.bfloat16)
    return (back, jnp.stack([first[1], second[1]]), jnp.stack([first[2], second[2]]),
            jnp.stack([first[3], second[3]]))


def reference(expert_inputs, routes, gate_prob, out_grad, gate_weight, up_weight, down_weight):
    expert_ids = jnp.arange(EXPERTS, dtype=jnp.int32)
    source_index = jnp.arange(N_EXPERT, dtype=jnp.int32)[:, None]
    upstream_list = [out_grad[number] for number in range(MB)]
    section_inputs = [None] * N_PIPE
    gate_out = [None] * N_PIPE
    up_out = [None] * N_PIPE
    down_out = [None] * N_PIPE
    for section_number in range(N_PIPE - 1, -1, -1):
        gate_cols = gate_weight[section_number].reshape(D, EXPERTS, 2, HID_DEV).transpose(1, 2, 0, 3)
        up_cols = up_weight[section_number].reshape(D, EXPERTS, 2, HID_DEV).transpose(1, 2, 0, 3)
        down_rows = down_weight[section_number].reshape(EXPERTS, 2, HID_DEV, D)
        acc_gate = jnp.zeros((EXPERTS, 2, D, HID_DEV), jnp.float32)
        acc_up = jnp.zeros((EXPERTS, 2, D, HID_DEV), jnp.float32)
        acc_down = jnp.zeros((EXPERTS, 2, HID_DEV, D), jnp.float32)
        new_list = []
        for micro_batch in range(MB):
            upstream = upstream_list[micro_batch]
            route_rows = routes[section_number, micro_batch].reshape(N_EXPERT, TOK_DEV * TOP).astype(jnp.int32)
            gate_probs = gate_prob[section_number, micro_batch].reshape(N_EXPERT, TOK_DEV, TOP)
            blocks = upstream.reshape(N_EXPERT, TOK_DEV, 1, D).astype(jnp.float32)
            scaled = (gate_probs[..., None] * blocks).astype(jnp.bfloat16).reshape(N_EXPERT, TOK_DEV * TOP, D)
            member = (route_rows[..., None] == expert_ids).astype(jnp.int32)
            rank_of = jnp.sum((jnp.cumsum(member, axis=1, dtype=jnp.int32) - 1) * member, axis=2).astype(jnp.int32)
            slot_of = (route_rows * CAP + rank_of).astype(jnp.int32)
            buffers = jnp.zeros((N_EXPERT, EXPERTS * CAP, D), jnp.bfloat16).at[source_index, slot_of].set(scaled)
            expert_rows = buffers.reshape(N_EXPERT, EXPERTS, CAP, D).transpose(1, 0, 2, 3).reshape(EXPERTS, N_EXPERT * CAP, D)
            saved_rows = expert_inputs[section_number, micro_batch].reshape(EXPERTS, 2, N_EXPERT, HALF, D)
            saved_rows = saved_rows.transpose(0, 2, 1, 3, 4).reshape(EXPERTS, N_EXPERT * CAP, D)
            backs, grad_gate, grad_up, grad_down = lax.map(
                per_expert, (expert_rows, saved_rows, gate_cols, up_cols, down_rows))
            acc_gate = acc_gate + grad_gate
            acc_up = acc_up + grad_up
            acc_down = acc_down + grad_down
            back_slots = backs.reshape(EXPERTS, N_EXPERT, CAP, D).transpose(1, 0, 2, 3).reshape(N_EXPERT, EXPERTS * CAP, D)
            back_tok = jnp.take_along_axis(back_slots, slot_of[..., None], axis=1).astype(jnp.float32)
            back_tok = back_tok.reshape(N_EXPERT, TOK_DEV, TOP, D).sum(axis=2)
            result = (blocks[:, :, 0, :] + back_tok).astype(jnp.bfloat16).reshape(TOKENS, D)
            new_list.append(result)
        upstream_list = new_list
        section_inputs[section_number] = jnp.stack(new_list)
        gate_out[section_number] = acc_gate.transpose(2, 0, 1, 3).reshape(D, EXPERTS * HID).astype(jnp.bfloat16)
        up_out[section_number] = acc_up.transpose(2, 0, 1, 3).reshape(D, EXPERTS * HID).astype(jnp.bfloat16)
        down_out[section_number] = acc_down.reshape(EXPERTS * HID, D).astype(jnp.bfloat16)
    return (jnp.stack(section_inputs), jnp.stack(gate_out), jnp.stack(up_out), jnp.stack(down_out))
```

```python
import functools

import jax
import jax.numpy as jnp
import numpy as np
from jax import lax
from jax.experimental import pallas as pl
from jax.experimental.pallas import tpu as pltpu
from jax.sharding import PartitionSpec as P

MESH = pl.DeviceIdType.MESH
F32 = jnp.float32
BF16 = jnp.bfloat16


def dot(left, right, left_dim, right_dim):
    return lax.dot_general(
        left, right, (((left_dim,), (right_dim,)), ((), ())), preferred_element_type=F32
    )


def row_order(chips, half):
    cap = 2 * half
    side = chips * cap
    order = np.zeros((2 * side, 2 * side), np.float32)
    for core in range(2):
        for chip in range(chips):
            for c in range(cap):
                source = (c // half) * side + (2 * chip + core) * half + c % half
                order[core * side + chip * cap + c, source] = 1.0
    return order


def kernel(
    sections,
    chips,
    cap,
    steps,
    route_ref,
    prob_ref,
    order_ref,
    saved_hbm,
    grad_hbm,
    wg_hbm,
    wu_hbm,
    wd_hbm,
    out_hbm,
    gg_hbm,
    gu_hbm,
    gd_hbm,
    wg,
    wu,
    wd,
    gg,
    gu,
    gd,
    saved,
    savedp,
    rows,
    parts,
    theirs,
    snd1,
    rcv1,
    snd2,
    rcv2,
    up,
    res,
    place,
    place_t,
    pre_g,
    pre_u,
    dh,
    deltas,
    hidden,
    in_sem,
    out_sem,
    sx_sem,
    d1_send,
    d1_recv,
    d1_own,
    rx_send,
    rx_recv,
    px_send,
    px_recv,
    d2_send,
    d2_recv,
    d2_own,
    z_send,
    z_recv,
):
    section = lax.axis_index("pipe")
    me = lax.axis_index("expert")
    chip = me // 2
    core = me % 2
    side = chips * cap
    features = up.shape[1]
    units = wg.shape[1]
    width = features // steps
    lanes = width // 128
    partner = (section, 2 * chip + 1 - core)
    below = (lax.rem(section + sections - 1, sections), me)
    above = (lax.rem(section + 1, sections), me)
    far = side - cap

    def cols(d):
        return pl.ds(pl.multiple_of(d * width, 128), width)

    def peer(k):
        other = lax.rem(chip + k, chips)
        return other, (section, 2 * other + core)

    barrier = pltpu.get_barrier_semaphore()
    for target in (partner, below, above):
        pl.semaphore_signal(barrier, inc=1, device_id=target, device_id_type=MESH)

    @pl.loop(1, chips)
    def _(k):
        pl.semaphore_signal(barrier, inc=1, device_id=peer(k)[1], device_id_type=MESH)

    loads = [
        pltpu.make_async_copy(saved_hbm, saved.at[core], in_sem.at[0]),
        pltpu.make_async_copy(wg_hbm.at[0], wg, in_sem.at[1]),
        pltpu.make_async_copy(wu_hbm.at[0], wu, in_sem.at[2]),
        pltpu.make_async_copy(wd_hbm.at[0], wd, in_sem.at[3]),
    ]
    first = pltpu.make_async_copy(grad_hbm.at[0], up, in_sem.at[4])
    is_first = section == sections - 1

    @pl.when(is_first)
    def _():
        first.start()

    for load in loads:
        load.start()

    tokens = route_ref.shape[0]
    member = (route_ref[...] == lax.broadcasted_iota(jnp.int32, (tokens, 128), 1)).astype(F32)
    earlier = (
        lax.broadcasted_iota(jnp.int32, (tokens, tokens), 1)
        < lax.broadcasted_iota(jnp.int32, (tokens, tokens), 0)
    ).astype(BF16)
    before = dot(earlier, member.astype(BF16), 1, 0)
    rank = jnp.sum(before * member, axis=1, keepdims=True)
    slot = route_ref[...].astype(F32) * cap + rank
    slots = lax.broadcasted_iota(jnp.int32, (tokens, side), 1).astype(F32)
    to_slot = (slot == slots).astype(F32)
    place_t[...] = to_slot.astype(BF16)
    place[...] = to_slot.T.astype(BF16)

    pl.semaphore_wait(barrier, chips + 2)

    def a2a(src, dst, d, k, send, recv):
        other, target = peer(k)
        return pltpu.make_async_remote_copy(
            src_ref=src.at[d, pl.ds(other * cap, cap)],
            dst_ref=dst.at[d, pl.ds(chip * cap, cap)],
            send_sem=send.at[d],
            recv_sem=recv.at[d],
            device_id=target,
            device_id_type=MESH,
        )

    def a2a_all(src, dst, d, send, recv):
        return pltpu.make_async_remote_copy(
            src_ref=src.at[d, pl.ds(0, far)],
            dst_ref=dst.at[d, pl.ds(0, far)],
            send_sem=send.at[d],
            recv_sem=recv.at[d],
            device_id=partner,
            device_id_type=MESH,
        )

    def own(src, dst, d, sem):
        here = pl.ds(chip * cap, cap)
        return pltpu.make_async_copy(src.at[d, here], dst.at[d, here], sem.at[d])

    def spread(src, dst, d, send, recv, sem):
        own(src, dst, d, sem).start()

        @pl.loop(1, chips)
        def _(k):
            a2a(src, dst, d, k, send, recv).start()

    def collect(src, dst, d, send, recv, sem):
        own(src, dst, d, sem).wait()
        a2a_all(src, dst, d, send, recv).wait_recv()

    def rows_copy(d):
        return pltpu.make_async_remote_copy(
            src_ref=rows.at[core, :, cols(d)],
            dst_ref=rows.at[core, :, cols(d)],
            send_sem=rx_send.at[d],
            recv_sem=rx_recv.at[d],
            device_id=partner,
            device_id_type=MESH,
        )

    def rows_arrival(d):
        return pltpu.make_async_remote_copy(
            src_ref=rows.at[1 - core, :, cols(d)],
            dst_ref=rows.at[1 - core, :, cols(d)],
            send_sem=rx_send.at[d],
            recv_sem=rx_recv.at[d],
            device_id=partner,
            device_id_type=MESH,
        )

    def parts_copy(d):
        return pltpu.make_async_remote_copy(
            src_ref=parts.at[1 - core, :, cols(d)],
            dst_ref=theirs.at[:, cols(d)],
            send_sem=px_send.at[d],
            recv_sem=px_recv.at[d],
            device_id=partner,
            device_id_type=MESH,
        )

    def down_copy(d):
        return pltpu.make_async_remote_copy(
            src_ref=res.at[:, cols(d)],
            dst_ref=up.at[:, cols(d)],
            send_sem=z_send.at[d],
            recv_sem=z_recv.at[d],
            device_id=below,
            device_id_type=MESH,
        )

    saved_copy = pltpu.make_async_remote_copy(
        src_ref=saved.at[core],
        dst_ref=saved.at[core],
        send_sem=sx_sem.at[0],
        recv_sem=sx_sem.at[1],
        device_id=partner,
        device_id_type=MESH,
    )
    saved_arrival = pltpu.make_async_remote_copy(
        src_ref=saved.at[1 - core],
        dst_ref=saved.at[1 - core],
        send_sem=sx_sem.at[0],
        recv_sem=sx_sem.at[1],
        device_id=partner,
        device_id_type=MESH,
    )

    def dispatch(d):
        scaled = (prob_ref[...] * up[:, cols(d)].astype(F32)).astype(BF16)
        placed = dot(place[...], scaled, 1, 0).astype(BF16)
        snd1[d] = placed.reshape(side, lanes, 128)
        spread(snd1, rcv1, d, d1_send, d1_recv, d1_own)

    def take(d):
        collect(snd1, rcv1, d, d1_send, d1_recv, d1_own)
        rows[core, :, cols(d)] = rcv1[d].reshape(side, width)
        rows_copy(d).start()

    def add_hidden(d):
        rows_arrival(d).wait_recv()
        both = rows[:, :, cols(d)].reshape(2 * side, width)
        dh[...] += dot(both, wd[:, cols(d)], 1, 1)

    def forward():
        loads[1].wait()
        loads[2].wait()
        saved_arrival.wait_recv()
        pre_g[...] = jnp.zeros_like(pre_g)
        pre_u[...] = jnp.zeros_like(pre_u)

        @pl.loop(0, steps)
        def _(d):
            mixed = saved[:, :, cols(d)].reshape(2 * side, width)
            now = dot(order_ref[...], mixed, 1, 0).astype(BF16)
            savedp[:, cols(d)] = now
            pre_g[...] += dot(now, wg[cols(d), :], 1, 0)
            pre_u[...] += dot(now, wu[cols(d), :], 1, 0)

        gate = pre_g[...]
        pre_up = pre_u[...]
        sigmoid = jax.nn.sigmoid(gate)
        silu = gate * sigmoid
        hidden[...] = (silu * pre_up).astype(BF16)
        pre_u[...] = silu
        pre_g[...] = pre_up * sigmoid * (1.0 + gate * (1.0 - sigmoid))
        loads[3].wait()

    def part(d):
        both = dot(deltas[:, :units], wg[cols(d), :], 1, 1)
        both += dot(deltas[:, units:], wu[cols(d), :], 1, 1)
        parts[:, :, cols(d)] = both.astype(BF16).reshape(2, side, width)
        parts_copy(d).start()

    def give(d):
        parts_copy(d).wait_recv()
        back = parts[core, :, cols(d)].astype(F32) + theirs[:, cols(d)].astype(F32)
        snd2[d] = back.astype(BF16).reshape(side, lanes, 128)
        spread(snd2, rcv2, d, d2_send, d2_recv, d2_own)

    def finish(d):
        collect(snd2, rcv2, d, d2_send, d2_recv, d2_own)
        back = dot(place_t[...], rcv2[d].reshape(side, width), 1, 0)
        res[:, cols(d)] = (up[:, cols(d)].astype(F32) + back).astype(BF16)

        @pl.when(section > 0)
        def _():
            down_copy(d).start()

    def weight_grads():
        @pl.loop(0, steps)
        def _(d):
            here = cols(d)
            both = dot(savedp[:, here], deltas[...], 0, 0).astype(BF16)
            gg[here, :] = both[:, :units]
            gu[here, :] = both[:, units:]
            grad_rows = rows[:, :, here].reshape(2 * side, width)
            gd[:, here] = dot(hidden[...], grad_rows, 0, 0).astype(BF16)
            pltpu.make_async_copy(gg.at[here], gg_hbm.at[0, here], out_sem.at[1]).start()
            pltpu.make_async_copy(gu.at[here], gu_hbm.at[0, here], out_sem.at[2]).start()
            pltpu.make_async_copy(gd.at[:, here], gd_hbm.at[0, :, here], out_sem.at[3]).start()

    dh[...] = jnp.zeros_like(dh)
    loads[0].wait()

    @pl.when(is_first)
    def _():
        first.wait()
        pl.loop(0, steps)(dispatch)

    saved_copy.start()
    forward()

    @pl.loop(0, steps + 2)
    def _(d):
        @pl.when((d < steps) & (section < sections - 1))
        def _():
            down_copy(d).wait_recv()
            dispatch(d)

        @pl.when((d >= 1) & (d < steps + 1))
        def _():
            take(d - 1)

        @pl.when(d >= 2)
        def _():
            add_hidden(d - 2)

    delta = dh[...]
    deltas[:, :units] = (delta * pre_g[...]).astype(BF16)
    deltas[:, units:] = (delta * pre_u[...]).astype(BF16)

    @pl.loop(0, steps + 1)
    def _(d):
        @pl.when(d < steps)
        def _():
            part(d)

        @pl.when(d >= 1)
        def _():
            give(d - 1)

    @pl.when(section == 0)
    def _():
        weight_grads()

    pl.loop(0, steps)(finish)
    result = pltpu.make_async_copy(res, out_hbm.at[0, 0], out_sem.at[0])
    result.start()

    @pl.when(section > 0)
    def _():
        weight_grads()

    saved_copy.wait_send()

    @pl.loop(0, steps)
    def _(d):
        a2a_all(snd1, rcv1, d, d1_send, d1_recv).wait_send()
        a2a_all(snd2, rcv2, d, d2_send, d2_recv).wait_send()
        rows_copy(d).wait_send()
        parts_copy(d).wait_send()

        @pl.when(section > 0)
        def _():
            down_copy(d).wait_send()

    result.wait()
    pltpu.make_async_copy(gg, gg_hbm.at[0], out_sem.at[1]).wait()
    pltpu.make_async_copy(gu, gu_hbm.at[0], out_sem.at[2]).wait()
    pltpu.make_async_copy(gd, gd_hbm.at[0], out_sem.at[3]).wait()


def body(expert_inputs, routes, gate_prob, out_grad, gate_weight, up_weight, down_weight):
    sections = lax.axis_size("pipe")
    members = lax.axis_size("expert")
    chips = members // 2
    tokens, features = out_grad.shape[1:]
    half = expert_inputs.shape[4]
    cap = 2 * half
    units = gate_weight.shape[2]
    side = chips * cap
    steps = 4
    lanes = features // steps // 128
    saved = expert_inputs.reshape(side, features)
    order = jnp.asarray(row_order(chips, half), BF16)
    vmem = pl.BlockSpec(memory_space=pltpu.VMEM)
    hbm = pl.BlockSpec(memory_space=pl.ANY)
    dma = pltpu.SemaphoreType.DMA
    moved = pltpu.VMEM((steps, side, lanes, 128), BF16)
    square = pltpu.VMEM((2 * side, units), F32)
    return pl.pallas_call(
        functools.partial(kernel, sections, chips, cap, steps),
        out_shape=(
            jax.ShapeDtypeStruct((1, 1, tokens, features), BF16),
            jax.ShapeDtypeStruct((1, features, units), BF16),
            jax.ShapeDtypeStruct((1, features, units), BF16),
            jax.ShapeDtypeStruct((1, units, features), BF16),
        ),
        in_specs=[vmem] * 3 + [hbm] * 5,
        out_specs=(hbm,) * 4,
        scratch_shapes=[
            pltpu.VMEM((features, units), BF16),
            pltpu.VMEM((features, units), BF16),
            pltpu.VMEM((units, features), BF16),
            pltpu.VMEM((features, units), BF16),
            pltpu.VMEM((features, units), BF16),
            pltpu.VMEM((units, features), BF16),
            pltpu.VMEM((2, side, features), BF16),
            pltpu.VMEM((2 * side, features), BF16),
            pltpu.VMEM((2, side, features), BF16),
            pltpu.VMEM((2, side, features), BF16),
            pltpu.VMEM((side, features), BF16),
            moved,
            moved,
            moved,
            moved,
            pltpu.VMEM((tokens, features), BF16),
            pltpu.VMEM((tokens, features), BF16),
            pltpu.VMEM((side, tokens), BF16),
            pltpu.VMEM((tokens, side), BF16),
            square,
            square,
            square,
            pltpu.VMEM((2 * side, 2 * units), BF16),
            pltpu.VMEM((2 * side, units), BF16),
            dma((5,)),
            dma((4,)),
            dma((2,)),
        ]
        + [dma((steps,))] * 12,
        compiler_params=pltpu.CompilerParams(
            collective_id=0, has_side_effects=True, vmem_limit_bytes=58 * 2**20
        ),
    )(
        routes.reshape(tokens, 1),
        gate_prob.reshape(tokens, 1),
        order,
        saved,
        out_grad,
        gate_weight,
        up_weight,
        down_weight,
    )


def solution(mesh):
    return jax.shard_map(
        body,
        mesh=mesh,
        in_specs=(
            P("pipe", None, "expert", None, None, None),
            P("pipe", None, "expert", None),
            P("pipe", None, "expert", None),
            P(None, "expert", None),
            P("pipe", None, "expert"),
            P("pipe", None, "expert"),
            P("pipe", "expert", None),
        ),
        out_specs=(
            P("pipe", None, "expert", None),
            P("pipe", None, "expert"),
            P("pipe", None, "expert"),
            P("pipe", "expert", None),
        ),
        check_vma=False,
    )
```

```python
import functools

import jax
import jax.numpy as jnp
import numpy as np
from jax import lax
from jax.experimental import pallas as pl
from jax.experimental.pallas import tpu as pltpu
from jax.sharding import PartitionSpec as P

MESH = pl.DeviceIdType.MESH
F32 = jnp.float32
BF16 = jnp.bfloat16


def dot(left, right, left_dim, right_dim):
    return lax.dot_general(
        left, right, (((left_dim,), (right_dim,)), ((), ())), preferred_element_type=F32
    )


def row_order(chips, half):
    cap = 2 * half
    side = chips * cap
    order = np.zeros((2 * side, 2 * side), np.float32)
    for core in range(2):
        for chip in range(chips):
            for c in range(cap):
                source = (c // half) * side + (c % half) * 2 * chips + 2 * chip + core
                order[core * side + chip * cap + c, source] = 1.0
    return order


def relay(
    sections,
    chips,
    cap,
    steps,
    route_ref,
    prob_ref,
    order_ref,
    saved_hbm,
    grad_hbm,
    wg_hbm,
    wu_hbm,
    wd_hbm,
    out_hbm,
    savedp_hbm,
    rows_hbm,
    deltas_hbm,
    hidden_hbm,
    wg,
    wu,
    wd,
    saved,
    savedp,
    rows,
    parts,
    theirs,
    snd1,
    rcv1,
    snd2,
    rcv2,
    raw,
    up,
    res,
    fin,
    place,
    place_up,
    place_t,
    mix,
    psnd,
    prcv,
    prob_of,
    pre_g,
    pre_u,
    dh,
    deltas,
    hidden,
    in_sem,
    out_sem,
    sx_sem,
    d1_send,
    d1_recv,
    d1_own,
    rx_send,
    rx_recv,
    px_send,
    px_recv,
    d2_send,
    d2_recv,
    d2_own,
    z_send,
    z_recv,
    p_sem,
    q_sem,
):
    section = lax.axis_index("pipe")
    me = lax.axis_index("expert")
    chip = me // 2
    core = me % 2
    side = chips * cap
    features = up.shape[1]
    units = wg.shape[1]
    width = features // steps
    lanes = width // 128
    partner = (section, 2 * chip + 1 - core)
    is_first = section == sections - 1
    is_last = section == 0
    below = (lax.rem(section + sections - 1, sections), me)
    above = (lax.rem(section + 1, sections), me)
    far = side - cap

    def cols(d):
        return pl.ds(pl.multiple_of(d * width, 128), width)

    depth = min(4, chips)
    height = chips // depth
    offsets = sorted(
        ((i, j) for i in range(height) for j in range(depth)),
        key=lambda o: -min(o[0], height - o[0]) - min(o[1], depth - o[1]),
    )
    others = [
        lax.rem(chip // depth + i, height) * depth + lax.rem(chip % depth + j, depth)
        for i, j in offsets
    ]

    barrier = pltpu.get_barrier_semaphore()

    def greet(target):
        pl.semaphore_signal(barrier, inc=1, device_id=target, device_id_type=MESH)

    greet(partner)

    for other in others[:-1]:
        greet((section, 2 * other + core))

    @pl.when(jnp.logical_not(is_first))
    def _():
        for other in others:
            greet((above[0], 2 * other + core))

    @pl.when(jnp.logical_not(is_last))
    def _():
        for other in others:
            greet((below[0], 2 * other + core))

    loads = [
        pltpu.make_async_copy(saved_hbm, saved.at[core], in_sem.at[0]),
        pltpu.make_async_copy(wg_hbm.at[0], wg, in_sem.at[1]),
        pltpu.make_async_copy(wu_hbm.at[0], wu, in_sem.at[2]),
        pltpu.make_async_copy(wd_hbm.at[0], wd, in_sem.at[3]),
    ]
    first = pltpu.make_async_copy(grad_hbm.at[0], up, in_sem.at[4])

    @pl.when(is_first)
    def _():
        first.start()

    for load in loads:
        load.start()

    tokens = route_ref.shape[1]
    experts = lax.broadcasted_iota(jnp.int32, (max(chips, 8), tokens), 0)
    member = (route_ref[...] == experts).astype(F32)
    earlier = (
        lax.broadcasted_iota(jnp.int32, (tokens, tokens), 0)
        < lax.broadcasted_iota(jnp.int32, (tokens, tokens), 1)
    )
    before = dot(member.astype(BF16), earlier.astype(BF16), 1, 0)
    rank = jnp.sum(before * member, axis=0, keepdims=True)
    slot = route_ref[...].astype(F32) * cap + rank
    slots = lax.broadcasted_iota(jnp.int32, (side, tokens), 0).astype(F32)
    to_slot = (slot == slots).astype(F32)
    place[...] = to_slot.astype(BF16)
    prob_slot = jnp.sum(to_slot * prob_ref[...], axis=1, keepdims=True)
    psnd[...] = jnp.broadcast_to(prob_slot, (side, 128)).reshape(side, 1, 128)

    pl.semaphore_wait(barrier, jnp.where(is_first | is_last, 2 * chips, 3 * chips))

    def piece(src, dst, target, send_sem, recv_sem):
        return pltpu.make_async_remote_copy(
            src_ref=src,
            dst_ref=dst,
            send_sem=send_sem,
            recv_sem=recv_sem,
            device_id=target,
            device_id_type=MESH,
        )

    mine = pl.ds(chip * cap, cap)
    most = pl.ds(0, far)

    def spread(src, dst, send, recv, keep):
        pltpu.make_async_copy(src.at[mine], dst.at[mine], keep).start()

        for other in others[:-1]:
            target = (section, 2 * other + core)
            piece(src.at[pl.ds(other * cap, cap)], dst.at[mine], target, send, recv).start()

    def collect(src, dst, send, recv, keep):
        pltpu.make_async_copy(src.at[mine], dst.at[mine], keep).wait()
        piece(src.at[most], dst.at[most], partner, send, recv).wait_recv()

    def spread_done(src, send, recv):
        piece(src.at[most], src.at[most], partner, send, recv).wait_send()

    def to_partner(src, dst, send_sem, recv_sem):
        return piece(src, dst, partner, send_sem, recv_sem)

    def rows_copy(p, d):
        here = rows.at[p, :, cols(d)]
        return to_partner(here, here, rx_send.at[d], rx_recv.at[d])

    def parts_copy(p, d):
        return to_partner(
            parts.at[p, :, cols(d)], theirs.at[:, cols(d)], px_send.at[d], px_recv.at[d]
        )

    def saved_copy(half):
        return to_partner(saved.at[half], saved.at[half], sx_sem.at[0], sx_sem.at[1])

    place_copy = piece(place, place_up, below, q_sem.at[0], q_sem.at[1])

    def up_copy(d):
        return piece(res.at[:, cols(d)], fin.at[:, cols(d)], above, z_send.at[d], z_recv.at[d])

    def dispatch(d):
        @pl.when(is_first)
        def _():
            placed = dot(place[...], up[:, cols(d)], 1, 0).astype(BF16)
            snd1[d] = placed.reshape(side, lanes, 128)

        @pl.when(jnp.logical_not(is_first))
        def _():
            piece(snd2.at[d], rcv2.at[0, d], above, d2_send.at[d], d2_recv.at[0, d]).wait_recv()
            moved = dot(mix[...], rcv2[0, d].reshape(side, width), 1, 0).astype(BF16)
            snd1[d] = moved.reshape(side, lanes, 128)

        spread(snd1.at[d], rcv1.at[d], d1_send.at[d], d1_recv.at[d], d1_own.at[d])

    def assemble(d):
        res[:, cols(d)] = dot(place_t[...], rcv2[0, d].reshape(side, width), 1, 0).astype(BF16)
        up_copy(d).start()

    def take(p, d):
        collect(snd1.at[d], rcv1.at[d], d1_send.at[d], d1_recv.at[d], d1_own.at[d])
        now = rcv1[d].reshape(side, width)
        raw[:, cols(d)] = now
        rows[p, :, cols(d)] = (prob_of[:, :1] * now.astype(F32)).astype(BF16)
        rows_copy(p, d).start()

    def add_hidden(p, d):
        dh[...] += dot(rows[p, :, cols(d)], wd[:, cols(d)], 1, 1)

    def forward():
        loads[1].wait()
        loads[2].wait()
        saved_copy(1 - core).wait_recv()
        pre_g[...] = jnp.zeros_like(pre_g)
        pre_u[...] = jnp.zeros_like(pre_u)

        @pl.loop(0, steps)
        def _(d):
            mixed = saved[:, :, cols(d)].reshape(2 * side, width)
            now = dot(order_ref[...], mixed, 1, 0).astype(BF16)
            savedp[:, cols(d)] = now
            pre_g[...] += dot(now, wg[cols(d), :], 1, 0).reshape(2, side, units)
            pre_u[...] += dot(now, wu[cols(d), :], 1, 0).reshape(2, side, units)

        gate = pre_g[...]
        pre_up = pre_u[...]
        sigmoid = jax.nn.sigmoid(gate)
        silu = gate * sigmoid
        hidden[...] = (silu * pre_up).astype(BF16)
        pre_u[...] = silu
        pre_g[...] = pre_up * sigmoid * (1.0 + gate * (1.0 - sigmoid))
        loads[3].wait()

    def make_deltas(p):
        delta = dh[...]
        deltas[p, :, :units] = (delta * pre_g[p]).astype(BF16)
        deltas[p, :, units:] = (delta * pre_u[p]).astype(BF16)
        for copy in saves(p):
            copy.start()

    def saves(p):
        return (
            pltpu.make_async_copy(rows.at[p], rows_hbm.at[p], out_sem.at[3 + 2 * p]),
            pltpu.make_async_copy(deltas.at[p], deltas_hbm.at[p], out_sem.at[4 + 2 * p]),
        )

    def part(p, d):
        both = dot(deltas[p, :, :units], wg[cols(d), :], 1, 1)
        both += dot(deltas[p, :, units:], wu[cols(d), :], 1, 1)
        parts[p, :, cols(d)] = both.astype(BF16)

    def give(p, d):
        parts_copy(p, d).wait_recv()
        back = parts[p, :, cols(d)].astype(F32) + theirs[:, cols(d)].astype(F32)
        total = raw[:, cols(d)].astype(F32) + back.astype(BF16).astype(F32)
        snd2[d] = total.astype(BF16).reshape(side, lanes, 128)

        @pl.when(jnp.logical_not(is_last))
        def _():
            for other in others:
                piece(
                    snd2.at[d, pl.ds(other * cap, cap)],
                    rcv2.at[0, d, mine],
                    (below[0], 2 * other + core),
                    d2_send.at[d],
                    d2_recv.at[0, d],
                ).start()

        @pl.when(is_last)
        def _():
            spread(snd2.at[d], rcv2.at[1, d], d2_send.at[d], d2_recv.at[1, d], d2_own.at[d])

    def finish(d):
        collect(snd2.at[d], rcv2.at[1, d], d2_send.at[d], d2_recv.at[1, d], d2_own.at[d])
        fin[:, cols(d)] = dot(place[...], rcv2[1, d].reshape(side, width), 0, 0).astype(BF16)

    loads[0].wait()
    saved_copy(core).start()
    ahead = is_first & (core == 0)

    @pl.when(jnp.logical_not(is_last))
    def _():
        place_copy.start()

    spread(psnd, prcv, p_sem.at[0], p_sem.at[1], p_sem.at[2])

    @pl.when(is_first)
    def _():
        first.wait()

    @pl.when(ahead)
    def _():
        pl.loop(0, steps)(dispatch)

    forward()
    collect(psnd, prcv, p_sem.at[0], p_sem.at[1], p_sem.at[2])
    prob_of[...] = prcv[...].reshape(side, 128)

    @pl.when(jnp.logical_not(is_first))
    def _():
        place_copy.wait_recv()
        mix[...] = dot(place[...], place_up[...], 1, 1).astype(BF16)
        place_t[...] = place_up[...].astype(F32).T.astype(BF16)

    kept = (
        pltpu.make_async_copy(savedp, savedp_hbm, out_sem.at[1]),
        pltpu.make_async_copy(hidden, hidden_hbm, out_sem.at[2]),
    )
    for copy in kept:
        copy.start()
    result = pltpu.make_async_copy(fin, out_hbm.at[0, 0], out_sem.at[0])

    @pl.loop(0, 2)
    def _(p):
        dh[...] = jnp.zeros_like(dh)

        @pl.when(core == p)
        def _():
            @pl.loop(0, steps + 1)
            def _(d):
                @pl.when((d < steps) & jnp.logical_not(ahead))
                def _():
                    dispatch(d)

                @pl.when(d >= 1)
                def _():
                    take(p, d - 1)
                    add_hidden(p, d - 1)

                @pl.when((d < steps) & jnp.logical_not(is_first))
                def _():
                    assemble(d)

            make_deltas(p)

            @pl.loop(0, steps + 1)
            def _(d):
                @pl.when(d < steps)
                def _():
                    part(p, d)

                @pl.when(d >= 1)
                def _():
                    give(p, d - 1)

            @pl.when(is_last)
            def _():
                pl.loop(0, steps)(finish)

        @pl.when(core != p)
        def _():
            @pl.loop(0, steps)
            def _(d):
                rows_copy(p, d).wait_recv()
                add_hidden(p, d)

            make_deltas(p)

            @pl.loop(0, steps)
            def _(d):
                part(p, d)
                parts_copy(p, d).start()

    @pl.when(jnp.logical_not(is_last))
    def _():
        @pl.loop(0, steps)
        def _(d):
            up_copy(d).wait_recv()

    result.start()
    saved_copy(core).wait_send()
    spread_done(psnd, p_sem.at[0], p_sem.at[1])

    @pl.when(jnp.logical_not(is_last))
    def _():
        place_copy.wait_send()

    @pl.loop(0, steps)
    def _(d):
        spread_done(snd1.at[d], d1_send.at[d], d1_recv.at[d])
        rows_copy(core, d).wait_send()
        parts_copy(1 - core, d).wait_send()

        @pl.when(is_last)
        def _():
            spread_done(snd2.at[d], d2_send.at[d], d2_recv.at[1, d])

        @pl.when(jnp.logical_not(is_last))
        def _():
            piece(snd2.at[d], rcv2.at[0, d], below, d2_send.at[d], d2_recv.at[0, d]).wait_send()

        @pl.when(jnp.logical_not(is_first))
        def _():
            up_copy(d).wait_send()

    result.wait()
    for copy in (*kept, *saves(0), *saves(1)):
        copy.wait()


def weight_grads(
    units, near_ref, savedp_ref, rows_ref, deltas_ref, hidden_ref, out_ref, gg_ref, gu_ref, gd_ref
):
    out_ref[...] = near_ref[...]
    count = savedp_ref.shape[0]
    both = dot(savedp_ref[...], deltas_ref[...].reshape(count, 2 * units), 0, 0).astype(BF16)
    gg_ref[0] = both[:, :units]
    gu_ref[0] = both[:, units:]
    grad_rows = rows_ref[...].reshape(count, rows_ref.shape[2])
    gd_ref[0] = dot(hidden_ref[...].reshape(count, units), grad_rows, 0, 0).astype(BF16)


def body(expert_inputs, routes, gate_prob, out_grad, gate_weight, up_weight, down_weight):
    sections = lax.axis_size("pipe")
    members = lax.axis_size("expert")
    chips = members // 2
    tokens, features = out_grad.shape[1:]
    half = expert_inputs.shape[4]
    cap = 2 * half
    units = gate_weight.shape[2]
    side = chips * cap
    steps = 4
    lanes = features // steps // 128
    saved = expert_inputs[0, 0, 0].transpose(1, 0, 2).reshape(side, features)
    order = jnp.asarray(row_order(chips, half), BF16)
    vmem = pl.BlockSpec(memory_space=pltpu.VMEM)
    hbm = pl.BlockSpec(memory_space=pl.ANY)
    dma = pltpu.SemaphoreType.DMA
    moved = pltpu.VMEM((steps, side, lanes, 128), BF16)
    square = pltpu.VMEM((2, side, units), F32)
    near, savedp, rows, deltas, hidden = pl.pallas_call(
        functools.partial(relay, sections, chips, cap, steps),
        out_shape=(
            jax.ShapeDtypeStruct((1, 1, tokens, features), BF16),
            jax.ShapeDtypeStruct((2 * side, features), BF16),
            jax.ShapeDtypeStruct((2, side, features), BF16),
            jax.ShapeDtypeStruct((2, side, 2 * units), BF16),
            jax.ShapeDtypeStruct((2, side, units), BF16),
        ),
        in_specs=[vmem] * 3 + [hbm] * 5,
        out_specs=(hbm,) * 5,
        scratch_shapes=[
            pltpu.VMEM((features, units), BF16),
            pltpu.VMEM((features, units), BF16),
            pltpu.VMEM((units, features), BF16),
            pltpu.VMEM((2, side, features), BF16),
            pltpu.VMEM((2 * side, features), BF16),
            pltpu.VMEM((2, side, features), BF16),
            pltpu.VMEM((2, side, features), BF16),
            pltpu.VMEM((side, features), BF16),
            moved,
            moved,
            moved,
            pltpu.VMEM((2, steps, side, lanes, 128), BF16),
            pltpu.VMEM((side, features), BF16),
            pltpu.VMEM((tokens, features), BF16),
            pltpu.VMEM((tokens, features), BF16),
            pltpu.VMEM((tokens, features), BF16),
            pltpu.VMEM((side, tokens), BF16),
            pltpu.VMEM((side, tokens), BF16),
            pltpu.VMEM((tokens, side), BF16),
            pltpu.VMEM((side, side), BF16),
            pltpu.VMEM((side, 1, 128), F32),
            pltpu.VMEM((side, 1, 128), F32),
            pltpu.VMEM((side, 128), F32),
            square,
            square,
            pltpu.VMEM((side, units), F32),
            pltpu.VMEM((2, side, 2 * units), BF16),
            pltpu.VMEM((2, side, units), BF16),
            dma((5,)),
            dma((7,)),
            dma((2,)),
        ]
        + [dma((steps,))] * 8
        + [dma((2, steps))]
        + [dma((steps,))] * 3
        + [dma((3,)), dma((2,))],
        compiler_params=pltpu.CompilerParams(
            collective_id=0, has_side_effects=True, vmem_limit_bytes=58 * 2**20
        ),
    )(
        routes.reshape(1, tokens),
        gate_prob.reshape(1, tokens),
        order,
        saved,
        out_grad,
        gate_weight,
        up_weight,
        down_weight,
    )
    tiles = 4
    tile = features // tiles
    return pl.pallas_call(
        functools.partial(weight_grads, units),
        grid=(tiles,),
        in_specs=[
            pl.BlockSpec((1, 1, tokens, tile), lambda i: (0, 0, 0, i)),
            pl.BlockSpec((2 * side, tile), lambda i: (0, i)),
            pl.BlockSpec((2, side, tile), lambda i: (0, 0, i)),
            pl.BlockSpec((2, side, 2 * units), lambda i: (0, 0, 0)),
            pl.BlockSpec((2, side, units), lambda i: (0, 0, 0)),
        ],
        out_specs=(
            pl.BlockSpec((1, 1, tokens, tile), lambda i: (0, 0, 0, i)),
            pl.BlockSpec((1, tile, units), lambda i: (0, i, 0)),
            pl.BlockSpec((1, tile, units), lambda i: (0, i, 0)),
            pl.BlockSpec((1, units, tile), lambda i: (0, 0, i)),
        ),
        out_shape=(
            jax.ShapeDtypeStruct((1, 1, tokens, features), BF16),
            jax.ShapeDtypeStruct((1, features, units), BF16),
            jax.ShapeDtypeStruct((1, features, units), BF16),
            jax.ShapeDtypeStruct((1, units, features), BF16),
        ),
        compiler_params=pltpu.CompilerParams(vmem_limit_bytes=60 * 2**20),
    )(near, savedp, rows, deltas, hidden)


def solution(mesh):
    return jax.shard_map(
        body,
        mesh=mesh,
        in_specs=(
            P("pipe", None, "expert", None, None, None),
            P("pipe", None, "expert", None),
            P("pipe", None, "expert", None),
            P(None, "expert", None),
            P("pipe", None, "expert"),
            P("pipe", None, "expert"),
            P("pipe", "expert", None),
        ),
        out_specs=(
            P("pipe", None, "expert", None),
            P("pipe", None, "expert"),
            P("pipe", None, "expert"),
            P("pipe", "expert", None),
        ),
        check_vma=False,
    )
```

```python
import functools

import jax
import jax.numpy as jnp
import numpy as np
from jax import lax
from jax.experimental import pallas as pl
from jax.experimental.pallas import tpu as pltpu
from jax.sharding import PartitionSpec as P

MESH = pl.DeviceIdType.MESH
F32 = jnp.float32
BF16 = jnp.bfloat16


def dot(left, right, left_dim, right_dim):
    return lax.dot_general(
        left, right, (((left_dim,), (right_dim,)), ((), ())), preferred_element_type=F32
    )


def row_order(chips, half):
    cap = 2 * half
    side = chips * cap
    order = np.zeros((2 * side, 2 * side), np.float32)
    for core in range(2):
        for chip in range(chips):
            for c in range(cap):
                source = (c // half) * side + (c % half) * 2 * chips + 2 * chip + core
                order[core * side + chip * cap + c, source] = 1.0
    return order


def relay(
    sections,
    chips,
    cap,
    steps,
    route_ref,
    prob_ref,
    order_ref,
    saved_hbm,
    grad_hbm,
    wg_hbm,
    wu_hbm,
    wd_hbm,
    out_kept,
    savedp_kept,
    rows_kept,
    deltas_kept,
    hidden_kept,
    wg,
    wu,
    wd,
    saved,
    savedp,
    rows,
    snd1,
    rcv1,
    snd2,
    rcv2,
    raw,
    up,
    res,
    fin,
    place,
    place_up,
    place_t,
    mix,
    psnd,
    prcv,
    prob_of,
    pre_g,
    pre_u,
    dh,
    deltas,
    hidden,
    deltas_out,
    hidden_out,
    in_sem,
    out_sem,
    d1_send,
    d1_recv,
    d1_own,
    rx_send,
    rx_recv,
    x_send,
    x_recv,
    d2_send,
    d2_recv,
    d2_own,
    z_send,
    z_recv,
    p_sem,
    q_sem,
):
    section = lax.axis_index("pipe")
    me = lax.axis_index("expert")
    chip = me // 2
    core = me % 2
    side = chips * cap
    features = up.shape[1]
    units = wg.shape[2]
    width = features // steps
    lanes = width // 128
    partner = (section, 2 * chip + 1 - core)
    is_first = section == sections - 1
    is_last = section == 0
    below = (lax.rem(section + sections - 1, sections), me)
    above = (lax.rem(section + 1, sections), me)
    far = side - cap

    def cols(d):
        return pl.ds(pl.multiple_of(d * width, 128), width)

    depth = min(4, chips)
    height = chips // depth
    offsets = sorted(
        ((i, j) for i in range(height) for j in range(depth)),
        key=lambda o: -min(o[0], height - o[0]) - min(o[1], depth - o[1]),
    )
    others = [
        lax.rem(chip // depth + i, height) * depth + lax.rem(chip % depth + j, depth)
        for i, j in offsets
    ]

    barrier = pltpu.get_barrier_semaphore()

    def greet(target):
        pl.semaphore_signal(barrier, inc=1, device_id=target, device_id_type=MESH)

    greet(partner)

    for other in others[:-1]:
        greet((section, 2 * other + core))

    @pl.when(jnp.logical_not(is_first))
    def _():
        for other in others:
            greet((above[0], 2 * other + core))

    @pl.when(jnp.logical_not(is_last))
    def _():
        for other in others:
            greet((below[0], 2 * other + core))

    loads = [
        pltpu.make_async_copy(saved_hbm, saved.at[core], in_sem.at[0]),
        pltpu.make_async_copy(wg_hbm.at[0], wg.at[core], in_sem.at[1]),
        pltpu.make_async_copy(wu_hbm.at[0], wu.at[core], in_sem.at[2]),
        pltpu.make_async_copy(wd_hbm.at[0], wd.at[core], in_sem.at[3]),
    ]
    first = pltpu.make_async_copy(grad_hbm.at[0], up, in_sem.at[4])

    @pl.when(is_first)
    def _():
        first.start()

    for load in loads:
        load.start()

    tokens = route_ref.shape[1]
    experts = lax.broadcasted_iota(jnp.int32, (max(chips, 8), tokens), 0)
    member = (route_ref[...] == experts).astype(F32)
    earlier = (
        lax.broadcasted_iota(jnp.int32, (tokens, tokens), 0)
        < lax.broadcasted_iota(jnp.int32, (tokens, tokens), 1)
    )
    before = dot(member.astype(BF16), earlier.astype(BF16), 1, 0)
    rank = jnp.sum(before * member, axis=0, keepdims=True)
    slot = route_ref[...].astype(F32) * cap + rank
    slots = lax.broadcasted_iota(jnp.int32, (side, tokens), 0).astype(F32)
    to_slot = (slot == slots).astype(F32)
    place[...] = to_slot.astype(BF16)
    prob_slot = jnp.sum(to_slot * prob_ref[...], axis=1, keepdims=True)
    psnd[...] = jnp.broadcast_to(prob_slot, (side, 128)).reshape(side, 1, 128)

    pl.semaphore_wait(barrier, jnp.where(is_first | is_last, 2 * chips, 3 * chips))

    def piece(src, dst, target, send_sem, recv_sem):
        return pltpu.make_async_remote_copy(
            src_ref=src,
            dst_ref=dst,
            send_sem=send_sem,
            recv_sem=recv_sem,
            device_id=target,
            device_id_type=MESH,
        )

    mine = pl.ds(chip * cap, cap)
    most = pl.ds(0, far)

    def spread(src, dst, send, recv, keep):
        pltpu.make_async_copy(src.at[mine], dst.at[mine], keep).start()

        for other in others[:-1]:
            target = (section, 2 * other + core)
            piece(src.at[pl.ds(other * cap, cap)], dst.at[mine], target, send, recv).start()

    def collect(src, dst, send, recv, keep):
        pltpu.make_async_copy(src.at[mine], dst.at[mine], keep).wait()
        piece(src.at[most], dst.at[most], partner, send, recv).wait_recv()

    def spread_done(src, send, recv):
        piece(src.at[most], src.at[most], partner, send, recv).wait_send()

    def to_partner(src, dst, send_sem, recv_sem):
        return piece(src, dst, partner, send_sem, recv_sem)

    def rows_copy(p, d):
        here = rows.at[p, :, cols(d)]
        return to_partner(here, here, rx_send.at[d], rx_recv.at[d])

    def exchange(ref, at, number):
        return to_partner(ref.at[at], ref.at[at], x_send.at[number], x_recv.at[number])

    weights = ((wd, 3), (wg, 1), (wu, 2))

    def hand_over(src, dst, number):
        return to_partner(src, dst.at[core], x_send.at[number], x_recv.at[number])

    def arrival(dst, number):
        return to_partner(dst.at[1 - core], dst.at[1 - core], x_send.at[number], x_recv.at[number])

    place_copy = piece(place, place_up, below, q_sem.at[0], q_sem.at[1])

    def up_copy(d):
        return piece(res.at[:, cols(d)], fin.at[:, cols(d)], above, z_send.at[d], z_recv.at[d])

    def dispatch(d):
        @pl.when(is_first)
        def _():
            placed = dot(place[...], up[:, cols(d)], 1, 0).astype(BF16)
            snd1[d] = placed.reshape(side, lanes, 128)

        @pl.when(jnp.logical_not(is_first))
        def _():
            piece(snd2.at[d], rcv2.at[0, d], above, d2_send.at[d], d2_recv.at[0, d]).wait_recv()
            moved = dot(mix[...], rcv2[0, d].reshape(side, width), 1, 0).astype(BF16)
            snd1[d] = moved.reshape(side, lanes, 128)

        spread(snd1.at[d], rcv1.at[d], d1_send.at[d], d1_recv.at[d], d1_own.at[d])

    def assemble(d):
        res[:, cols(d)] = dot(place_t[...], rcv2[0, d].reshape(side, width), 1, 0).astype(BF16)
        up_copy(d).start()

    def take(d):
        collect(snd1.at[d], rcv1.at[d], d1_send.at[d], d1_recv.at[d], d1_own.at[d])
        now = rcv1[d].reshape(side, width)
        raw[:, cols(d)] = now
        scaled = (prob_of[:, :1] * now.astype(F32)).astype(BF16)
        rows[core, :, cols(d)] = scaled
        for half in range(2):
            dh[half] += dot(scaled, wd[half, :, cols(d)], 1, 1)
        rows_copy(core, d).start()

    def pre(half):
        @pl.loop(0, steps)
        def _(d):
            now = savedp[pl.ds(pl.multiple_of(core * side, 16), side), cols(d)]
            pre_g[half] += dot(now, wg[half, cols(d), :], 1, 0)
            pre_u[half] += dot(now, wu[half, cols(d), :], 1, 0)

        gate = pre_g[half]
        pre_up = pre_u[half]
        sigmoid = jax.nn.sigmoid(gate)
        silu = gate * sigmoid
        hidden[half] = (silu * pre_up).astype(BF16)
        pre_u[half] = silu
        pre_g[half] = pre_up * sigmoid * (1.0 + gate * (1.0 - sigmoid))

    def forward():
        exchange(saved, 1 - core, 0).wait_recv()
        pre_g[...] = jnp.zeros_like(pre_g)
        pre_u[...] = jnp.zeros_like(pre_u)

        @pl.loop(0, steps)
        def _(d):
            mixed = saved[:, :, cols(d)].reshape(2 * side, width)
            savedp[:, cols(d)] = dot(order_ref[...], mixed, 1, 0).astype(BF16)

        pre(core)
        exchange(wd, 1 - core, 3).wait_recv()

    def forward_rest():
        for ref, number in weights[1:]:
            exchange(ref, 1 - core, number).wait_recv()
        pre(1 - core)
        hidden_out[core] = hidden[core]
        hand_over(hidden.at[1 - core], hidden_out, 4).start()

    def make_deltas():
        for half in range(2):
            delta = dh[half]
            deltas[half, :, :units] = (delta * pre_g[half]).astype(BF16)
            deltas[half, :, units:] = (delta * pre_u[half]).astype(BF16)
        deltas_out[core] = deltas[core]
        hand_over(deltas.at[1 - core], deltas_out, 5).start()

    def saves(p):
        return (
            pltpu.make_async_copy(rows.at[p], rows_kept.at[p], out_sem.at[3 + 2 * p]),
            pltpu.make_async_copy(deltas_out.at[p], deltas_kept.at[p], out_sem.at[4 + 2 * p]),
        )

    def part(half, d):
        here = cols(d)
        both = dot(deltas[half, :, :units], wg[half, here, :], 1, 1)
        both += dot(deltas[half, :, units:], wu[half, here, :], 1, 1)
        return both.astype(BF16).astype(F32)

    def give(d):
        back = (part(0, d) + part(1, d)).astype(BF16)
        total = raw[:, cols(d)].astype(F32) + back.astype(F32)
        snd2[d] = total.astype(BF16).reshape(side, lanes, 128)

        @pl.when(jnp.logical_not(is_last))
        def _():
            for other in others:
                piece(
                    snd2.at[d, pl.ds(other * cap, cap)],
                    rcv2.at[0, d, mine],
                    (below[0], 2 * other + core),
                    d2_send.at[d],
                    d2_recv.at[0, d],
                ).start()

        @pl.when(is_last)
        def _():
            spread(snd2.at[d], rcv2.at[1, d], d2_send.at[d], d2_recv.at[1, d], d2_own.at[d])

    def finish(d):
        collect(snd2.at[d], rcv2.at[1, d], d2_send.at[d], d2_recv.at[1, d], d2_own.at[d])
        fin[:, cols(d)] = dot(place[...], rcv2[1, d].reshape(side, width), 0, 0).astype(BF16)

    @pl.when(jnp.logical_not(is_last))
    def _():
        place_copy.start()

    spread(psnd, prcv, p_sem.at[0], p_sem.at[1], p_sem.at[2])

    @pl.when(is_first)
    def _():
        first.wait()

        @pl.when(core == 0)
        def _():
            pl.loop(0, steps)(dispatch)

    loads[0].wait()
    exchange(saved, core, 0).start()
    for ref, number in weights:
        loads[number].wait()
        exchange(ref, core, number).start()

    forward()
    collect(psnd, prcv, p_sem.at[0], p_sem.at[1], p_sem.at[2])
    prob_of[...] = prcv[...].reshape(side, 128)

    @pl.when(jnp.logical_not(is_first))
    def _():
        forward_rest()
        place_copy.wait_recv()
        mix[...] = dot(place[...], place_up[...], 1, 1).astype(BF16)
        place_t[...] = place_up[...].astype(F32).T.astype(BF16)

    kept = (
        pltpu.make_async_copy(savedp, savedp_kept, out_sem.at[1]),
        pltpu.make_async_copy(hidden_out, hidden_kept, out_sem.at[2]),
    )
    kept[0].start()
    result = pltpu.make_async_copy(fin, out_kept.at[0, 0], out_sem.at[0])
    dh[...] = jnp.zeros_like(dh)

    def partners_share():
        @pl.when(jnp.logical_not(is_first & (core == 1)))
        def _():
            pl.loop(0, steps)(lambda d: rows_copy(1 - core, d).wait_recv())

        arrival(hidden_out, 4).wait_recv()
        arrival(deltas_out, 5).wait_recv()
        kept[1].start()
        for copy in saves(1 - core):
            copy.start()

    @pl.when(is_first & (core == 1))
    def _():
        pl.loop(0, steps)(lambda d: rows_copy(0, d).wait_recv())

    @pl.loop(0, steps + 1)
    def _(d):
        @pl.when((d < steps) & jnp.logical_not(is_first & (core == 0)))
        def _():
            dispatch(d)

        @pl.when(d >= 1)
        def _():
            take(d - 1)

        @pl.when((d < steps) & jnp.logical_not(is_first))
        def _():
            assemble(d)

    @pl.when(is_first)
    def _():
        forward_rest()

    make_deltas()
    pl.loop(0, steps)(give)
    for copy in saves(core):
        copy.start()

    @pl.when(core == 1)
    def _():
        partners_share()

    @pl.when(is_last)
    def _():
        pl.loop(0, steps)(finish)

    @pl.when(jnp.logical_not(is_last))
    def _():
        @pl.loop(0, steps)
        def _(d):
            up_copy(d).wait_recv()

    result.start()

    @pl.when(core == 0)
    def _():
        partners_share()

    spread_done(psnd, p_sem.at[0], p_sem.at[1])
    exchange(saved, core, 0).wait_send()
    for ref, number in weights:
        exchange(ref, core, number).wait_send()
    hand_over(hidden.at[1 - core], hidden_out, 4).wait_send()
    hand_over(deltas.at[1 - core], deltas_out, 5).wait_send()

    @pl.when(jnp.logical_not(is_last))
    def _():
        place_copy.wait_send()

    @pl.loop(0, steps)
    def _(d):
        spread_done(snd1.at[d], d1_send.at[d], d1_recv.at[d])
        rows_copy(core, d).wait_send()

        @pl.when(is_last)
        def _():
            spread_done(snd2.at[d], d2_send.at[d], d2_recv.at[1, d])

        @pl.when(jnp.logical_not(is_last))
        def _():
            piece(snd2.at[d], rcv2.at[0, d], below, d2_send.at[d], d2_recv.at[0, d]).wait_send()

        @pl.when(jnp.logical_not(is_first))
        def _():
            up_copy(d).wait_send()

    result.wait()
    for copy in (*kept, *saves(0), *saves(1)):
        copy.wait()


def weight_grads(
    units, near_ref, savedp_ref, rows_ref, deltas_ref, hidden_ref, out_ref, gg_ref, gu_ref, gd_ref
):
    count = savedp_ref.shape[0]
    tile = gd_ref.shape[2]
    here = pl.ds(pl.multiple_of(pl.program_id(0) * tile, 128), tile)
    out_ref[...] = near_ref[:, :, :, here]
    both = dot(savedp_ref[:, here], deltas_ref[...].reshape(count, 2 * units), 0, 0).astype(BF16)
    gg_ref[0] = both[:, :units]
    gu_ref[0] = both[:, units:]
    grad_rows = rows_ref[:, :, here].reshape(count, tile)
    gd_ref[0] = dot(hidden_ref[...].reshape(count, units), grad_rows, 0, 0).astype(BF16)


def body(expert_inputs, routes, gate_prob, out_grad, gate_weight, up_weight, down_weight):
    sections = lax.axis_size("pipe")
    members = lax.axis_size("expert")
    chips = members // 2
    tokens, features = out_grad.shape[1:]
    half = expert_inputs.shape[4]
    cap = 2 * half
    units = gate_weight.shape[2]
    side = chips * cap
    steps = 4
    lanes = features // steps // 128
    saved = expert_inputs[0, 0, 0].transpose(1, 0, 2).reshape(side, features)
    order = jnp.asarray(row_order(chips, half), BF16)
    vmem = pl.BlockSpec(memory_space=pltpu.VMEM)
    hbm = pl.BlockSpec(memory_space=pl.ANY)
    dma = pltpu.SemaphoreType.DMA
    moved = pltpu.VMEM((steps, side, lanes, 128), BF16)
    square = pltpu.VMEM((2, side, units), F32)
    near, savedp, rows, deltas, hidden = pl.pallas_call(
        functools.partial(relay, sections, chips, cap, steps),
        out_shape=(
            pltpu.VMEM((1, 1, tokens, features), BF16),
            pltpu.VMEM((2 * side, features), BF16),
            pltpu.VMEM((2, side, features), BF16),
            pltpu.VMEM((2, side, 2 * units), BF16),
            pltpu.VMEM((2, side, units), BF16),
        ),
        in_specs=[vmem] * 3 + [hbm] * 5,
        out_specs=(vmem,) * 5,
        scratch_shapes=[
            pltpu.VMEM((2, features, units), BF16),
            pltpu.VMEM((2, features, units), BF16),
            pltpu.VMEM((2, units, features), BF16),
            pltpu.VMEM((2, side, features), BF16),
            pltpu.VMEM((2 * side, features), BF16),
            pltpu.VMEM((2, side, features), BF16),
            moved,
            moved,
            moved,
            pltpu.VMEM((2, steps, side, lanes, 128), BF16),
            pltpu.VMEM((side, features), BF16),
            pltpu.VMEM((tokens, features), BF16),
            pltpu.VMEM((tokens, features), BF16),
            pltpu.VMEM((tokens, features), BF16),
            pltpu.VMEM((side, tokens), BF16),
            pltpu.VMEM((side, tokens), BF16),
            pltpu.VMEM((tokens, side), BF16),
            pltpu.VMEM((side, side), BF16),
            pltpu.VMEM((side, 1, 128), F32),
            pltpu.VMEM((side, 1, 128), F32),
            pltpu.VMEM((side, 128), F32),
            square,
            square,
            square,
            pltpu.VMEM((2, side, 2 * units), BF16),
            pltpu.VMEM((2, side, units), BF16),
            pltpu.VMEM((2, side, 2 * units), BF16),
            pltpu.VMEM((2, side, units), BF16),
            dma((5,)),
            dma((7,)),
        ]
        + [dma((steps,))] * 5
        + [dma((6,))] * 2
        + [dma((steps,))]
        + [dma((2, steps))]
        + [dma((steps,))] * 3
        + [dma((3,)), dma((2,))],
        compiler_params=pltpu.CompilerParams(
            collective_id=0, has_side_effects=True, vmem_limit_bytes=52 * 2**20
        ),
    )(
        routes.reshape(1, tokens),
        gate_prob.reshape(1, tokens),
        order,
        saved,
        out_grad,
        gate_weight,
        up_weight,
        down_weight,
    )
    tiles = 4
    tile = features // tiles
    return pl.pallas_call(
        functools.partial(weight_grads, units),
        grid=(tiles,),
        in_specs=[
            vmem,
            vmem,
            vmem,
            vmem,
            vmem,
        ],
        out_specs=(
            pl.BlockSpec((1, 1, tokens, tile), lambda i: (0, 0, 0, i)),
            pl.BlockSpec((1, tile, units), lambda i: (0, i, 0)),
            pl.BlockSpec((1, tile, units), lambda i: (0, i, 0)),
            pl.BlockSpec((1, units, tile), lambda i: (0, 0, i)),
        ),
        out_shape=(
            jax.ShapeDtypeStruct((1, 1, tokens, features), BF16),
            jax.ShapeDtypeStruct((1, features, units), BF16),
            jax.ShapeDtypeStruct((1, features, units), BF16),
            jax.ShapeDtypeStruct((1, units, features), BF16),
        ),
        compiler_params=pltpu.CompilerParams(vmem_limit_bytes=30 * 2**20),
    )(near, savedp, rows, deltas, hidden)


def solution(mesh):
    return jax.shard_map(
        body,
        mesh=mesh,
        in_specs=(
            P("pipe", None, "expert", None, None, None),
            P("pipe", None, "expert", None),
            P("pipe", None, "expert", None),
            P(None, "expert", None),
            P("pipe", None, "expert"),
            P("pipe", None, "expert"),
            P("pipe", "expert", None),
        ),
        out_specs=(
            P("pipe", None, "expert", None),
            P("pipe", None, "expert"),
            P("pipe", None, "expert"),
            P("pipe", "expert", None),
        ),
        check_vma=False,
    )
```

```python
import functools

import jax
import jax.numpy as jnp
import numpy as np
from jax import lax
from jax.experimental import pallas as pl
from jax.experimental.pallas import tpu as pltpu
from jax.sharding import PartitionSpec as P

MESH = pl.DeviceIdType.MESH
F32 = jnp.float32
BF16 = jnp.bfloat16


def dot(left, right, left_dim, right_dim):
    return lax.dot_general(
        left, right, (((left_dim,), (right_dim,)), ((), ())), preferred_element_type=F32
    )


def row_order(chips, half):
    cap = 2 * half
    side = chips * cap
    order = np.zeros((2 * side, 2 * side), np.float32)
    for core in range(2):
        for chip in range(chips):
            for c in range(cap):
                source = (c // half) * side + (c % half) * 2 * chips + 2 * chip + core
                order[core * side + chip * cap + c, source] = 1.0
    return order


def relay(
    sections,
    chips,
    cap,
    steps,
    route_ref,
    prob_ref,
    order_ref,
    saved_hbm,
    grad_hbm,
    wg_hbm,
    wu_hbm,
    wd_hbm,
    out_kept,
    savedp_kept,
    rows_kept,
    deltas_kept,
    hidden_kept,
    wg,
    wu,
    wd,
    saved,
    savedp,
    rows,
    snd1,
    rcv1,
    snd2,
    rcv2,
    raw,
    up,
    res,
    fin,
    place,
    place_up,
    place_t,
    mix,
    psnd,
    prcv,
    prob_of,
    pre_g,
    pre_u,
    dh,
    deltas,
    hidden,
    deltas_out,
    hidden_out,
    in_sem,
    out_sem,
    d1_send,
    d1_recv,
    d1_own,
    rx_send,
    rx_recv,
    x_send,
    x_recv,
    d2_send,
    d2_recv,
    d2_own,
    z_send,
    z_recv,
    p_sem,
    q_sem,
):
    section = lax.axis_index("pipe")
    me = lax.axis_index("expert")
    chip = me // 2
    core = me % 2
    side = chips * cap
    features = up.shape[1]
    units = wg.shape[2]
    width = features // steps
    lanes = width // 128
    partner = (section, 2 * chip + 1 - core)
    is_first = section == sections - 1
    is_last = section == 0
    below = (lax.rem(section + sections - 1, sections), me)
    above = (lax.rem(section + 1, sections), me)
    far = side - cap

    def cols(d):
        return pl.ds(pl.multiple_of(d * width, 128), width)

    depth = min(4, chips)
    height = chips // depth
    offsets = sorted(
        ((i, j) for i in range(height) for j in range(depth)),
        key=lambda o: -min(o[0], height - o[0]) - min(o[1], depth - o[1]),
    )
    others = [
        lax.rem(chip // depth + i, height) * depth + lax.rem(chip % depth + j, depth)
        for i, j in offsets
    ]

    barrier = pltpu.get_barrier_semaphore()

    def greet(target):
        pl.semaphore_signal(barrier, inc=1, device_id=target, device_id_type=MESH)

    greet(partner)

    for other in others[:-1]:
        greet((section, 2 * other + core))

    @pl.when(jnp.logical_not(is_first))
    def _():
        for other in others:
            greet((above[0], 2 * other + core))

    @pl.when(jnp.logical_not(is_last))
    def _():
        for other in others:
            greet((below[0], 2 * other + core))

    loads = [
        pltpu.make_async_copy(saved_hbm, saved.at[core], in_sem.at[0]),
        pltpu.make_async_copy(wg_hbm.at[0], wg.at[core], in_sem.at[1]),
        pltpu.make_async_copy(wu_hbm.at[0], wu.at[core], in_sem.at[2]),
        pltpu.make_async_copy(wd_hbm.at[0], wd.at[core], in_sem.at[3]),
    ]
    first = pltpu.make_async_copy(grad_hbm.at[0], up, in_sem.at[4])

    @pl.when(is_first)
    def _():
        first.start()

    for load in loads:
        load.start()

    tokens = route_ref.shape[1]
    experts = lax.broadcasted_iota(jnp.int32, (max(chips, 8), tokens), 0)
    member = (route_ref[...] == experts).astype(F32)
    earlier = (
        lax.broadcasted_iota(jnp.int32, (tokens, tokens), 0)
        < lax.broadcasted_iota(jnp.int32, (tokens, tokens), 1)
    )
    before = dot(member.astype(BF16), earlier.astype(BF16), 1, 0)
    rank = jnp.sum(before * member, axis=0, keepdims=True)
    slot = route_ref[...].astype(F32) * cap + rank
    slots = lax.broadcasted_iota(jnp.int32, (side, tokens), 0).astype(F32)
    to_slot = (slot == slots).astype(F32)
    place[...] = to_slot.astype(BF16)
    prob_slot = jnp.sum(to_slot * prob_ref[...], axis=1, keepdims=True)
    psnd[...] = jnp.broadcast_to(prob_slot, (side, 128)).reshape(side, 1, 128)

    pl.semaphore_wait(barrier, jnp.where(is_first | is_last, 2 * chips, 3 * chips))

    def piece(src, dst, target, send_sem, recv_sem):
        return pltpu.make_async_remote_copy(
            src_ref=src,
            dst_ref=dst,
            send_sem=send_sem,
            recv_sem=recv_sem,
            device_id=target,
            device_id_type=MESH,
        )

    mine = pl.ds(chip * cap, cap)
    most = pl.ds(0, far)

    def spread(src, dst, send, recv, keep):
        pltpu.make_async_copy(src.at[mine], dst.at[mine], keep).start()

        for other in others[:-1]:
            target = (section, 2 * other + core)
            piece(src.at[pl.ds(other * cap, cap)], dst.at[mine], target, send, recv).start()

    def collect(src, dst, send, recv, keep):
        pltpu.make_async_copy(src.at[mine], dst.at[mine], keep).wait()
        piece(src.at[most], dst.at[most], partner, send, recv).wait_recv()

    def spread_done(src, send, recv):
        piece(src.at[most], src.at[most], partner, send, recv).wait_send()

    def to_partner(src, dst, send_sem, recv_sem):
        return piece(src, dst, partner, send_sem, recv_sem)

    def rows_copy(p, d):
        here = rows.at[p, :, cols(d)]
        return to_partner(here, here, rx_send.at[d], rx_recv.at[d])

    def exchange(ref, at, number):
        return to_partner(ref.at[at], ref.at[at], x_send.at[number], x_recv.at[number])

    weights = ((wd, 3), (wg, 1), (wu, 2))

    def hand_over(src, dst, number):
        return to_partner(src, dst.at[core], x_send.at[number], x_recv.at[number])

    def arrival(dst, number):
        return to_partner(dst.at[1 - core], dst.at[1 - core], x_send.at[number], x_recv.at[number])

    place_copy = piece(place, place_up, below, q_sem.at[0], q_sem.at[1])

    def up_copy(d):
        return piece(res.at[:, cols(d)], fin.at[:, cols(d)], above, z_send.at[d], z_recv.at[d])

    def dispatch(d):
        @pl.when(is_first)
        def _():
            placed = dot(place[...], up[:, cols(d)], 1, 0).astype(BF16)
            snd1[d] = placed.reshape(side, lanes, 128)

        @pl.when(jnp.logical_not(is_first))
        def _():
            piece(snd2.at[d], rcv2.at[0, d], above, d2_send.at[d], d2_recv.at[0, d]).wait_recv()
            moved = dot(mix[...], rcv2[0, d].reshape(side, width), 1, 0).astype(BF16)
            snd1[d] = moved.reshape(side, lanes, 128)

        spread(snd1.at[d], rcv1.at[d], d1_send.at[d], d1_recv.at[d], d1_own.at[d])

    def assemble(d):
        res[:, cols(d)] = dot(place_t[...], rcv2[0, d].reshape(side, width), 1, 0).astype(BF16)
        up_copy(d).start()

    def take(d):
        collect(snd1.at[d], rcv1.at[d], d1_send.at[d], d1_recv.at[d], d1_own.at[d])
        now = rcv1[d].reshape(side, width)
        raw[:, cols(d)] = now
        scaled = (prob_of[:, :1] * now.astype(F32)).astype(BF16)
        rows[core, :, cols(d)] = scaled
        for half in range(2):
            dh[half] += dot(scaled, wd[half, :, cols(d)], 1, 1)
        rows_copy(core, d).start()

    def pre(half):
        @pl.loop(0, steps)
        def _(d):
            now = savedp[pl.ds(pl.multiple_of(core * side, 16), side), cols(d)]
            pre_g[half] += dot(now, wg[half, cols(d), :], 1, 0)
            pre_u[half] += dot(now, wu[half, cols(d), :], 1, 0)

        gate = pre_g[half]
        pre_up = pre_u[half]
        sigmoid = jax.nn.sigmoid(gate)
        silu = gate * sigmoid
        hidden[half] = (silu * pre_up).astype(BF16)
        pre_u[half] = silu
        pre_g[half] = pre_up * sigmoid * (1.0 + gate * (1.0 - sigmoid))

    def forward():
        exchange(saved, 1 - core, 0).wait_recv()
        pre_g[...] = jnp.zeros_like(pre_g)
        pre_u[...] = jnp.zeros_like(pre_u)

        @pl.loop(0, steps)
        def _(d):
            mixed = saved[:, :, cols(d)].reshape(2 * side, width)
            savedp[:, cols(d)] = dot(order_ref[...], mixed, 1, 0).astype(BF16)

        pre(core)
        exchange(wd, 1 - core, 3).wait_recv()

    def forward_rest():
        for ref, number in weights[1:]:
            exchange(ref, 1 - core, number).wait_recv()
        pre(1 - core)
        hidden_out[core] = hidden[core]
        hand_over(hidden.at[1 - core], hidden_out, 4).start()

    def make_deltas():
        for half in range(2):
            delta = dh[half]
            deltas[half, :, :units] = (delta * pre_g[half]).astype(BF16)
            deltas[half, :, units:] = (delta * pre_u[half]).astype(BF16)
        deltas_out[core] = deltas[core]
        hand_over(deltas.at[1 - core], deltas_out, 5).start()

    def saves(p):
        return (
            pltpu.make_async_copy(rows.at[p], rows_kept.at[p], out_sem.at[3 + 2 * p]),
            pltpu.make_async_copy(deltas_out.at[p], deltas_kept.at[p], out_sem.at[4 + 2 * p]),
        )

    def part(half, d):
        here = cols(d)
        both = dot(deltas[half, :, :units], wg[half, here, :], 1, 1)
        both += dot(deltas[half, :, units:], wu[half, here, :], 1, 1)
        return both.astype(BF16).astype(F32)

    def give(d):
        back = (part(0, d) + part(1, d)).astype(BF16)
        total = raw[:, cols(d)].astype(F32) + back.astype(F32)
        snd2[d] = total.astype(BF16).reshape(side, lanes, 128)

        @pl.when(jnp.logical_not(is_last))
        def _():
            for other in others:
                piece(
                    snd2.at[d, pl.ds(other * cap, cap)],
                    rcv2.at[0, d, mine],
                    (below[0], 2 * other + core),
                    d2_send.at[d],
                    d2_recv.at[0, d],
                ).start()

        @pl.when(is_last)
        def _():
            spread(snd2.at[d], rcv2.at[1, d], d2_send.at[d], d2_recv.at[1, d], d2_own.at[d])

    def finish(d):
        collect(snd2.at[d], rcv2.at[1, d], d2_send.at[d], d2_recv.at[1, d], d2_own.at[d])
        fin[:, cols(d)] = dot(place[...], rcv2[1, d].reshape(side, width), 0, 0).astype(BF16)

    @pl.when(jnp.logical_not(is_last))
    def _():
        place_copy.start()

    spread(psnd, prcv, p_sem.at[0], p_sem.at[1], p_sem.at[2])

    @pl.when(is_first)
    def _():
        first.wait()

        @pl.when(core == 0)
        def _():
            pl.loop(0, steps)(dispatch)

    loads[0].wait()
    exchange(saved, core, 0).start()
    for ref, number in weights:
        loads[number].wait()
        exchange(ref, core, number).start()

    forward()
    collect(psnd, prcv, p_sem.at[0], p_sem.at[1], p_sem.at[2])
    prob_of[...] = prcv[...].reshape(side, 128)

    @pl.when(jnp.logical_not(is_first))
    def _():
        forward_rest()
        place_copy.wait_recv()
        mix[...] = dot(place[...], place_up[...], 1, 1).astype(BF16)
        place_t[...] = place_up[...].astype(F32).T.astype(BF16)

    kept = (
        pltpu.make_async_copy(savedp, savedp_kept, out_sem.at[1]),
        pltpu.make_async_copy(hidden_out, hidden_kept, out_sem.at[2]),
    )
    kept[0].start()
    result = pltpu.make_async_copy(fin, out_kept.at[0, 0], out_sem.at[0])
    dh[...] = jnp.zeros_like(dh)

    def partners_share():
        @pl.when(jnp.logical_not(is_first & (core == 1)))
        def _():
            pl.loop(0, steps)(lambda d: rows_copy(1 - core, d).wait_recv())

        arrival(hidden_out, 4).wait_recv()
        arrival(deltas_out, 5).wait_recv()
        kept[1].start()
        for copy in saves(1 - core):
            copy.start()

    @pl.when(is_first & (core == 1))
    def _():
        pl.loop(0, steps)(lambda d: rows_copy(0, d).wait_recv())

    @pl.loop(0, steps + 3)
    def _(d):
        @pl.when((d < steps) & jnp.logical_not(is_first & (core == 0)))
        def _():
            dispatch(d)

        @pl.when((d < steps) & jnp.logical_not(is_first))
        def _():
            assemble(d)

        @pl.when(d >= 3)
        def _():
            take(d - 3)

    @pl.when(is_first)
    def _():
        forward_rest()

    make_deltas()
    pl.loop(0, steps)(give)
    for copy in saves(core):
        copy.start()

    @pl.when(core == 1)
    def _():
        partners_share()

    @pl.when(is_last)
    def _():
        pl.loop(0, steps)(finish)

    @pl.when(jnp.logical_not(is_last))
    def _():
        @pl.loop(0, steps)
        def _(d):
            up_copy(d).wait_recv()

    result.start()

    @pl.when(core == 0)
    def _():
        partners_share()

    spread_done(psnd, p_sem.at[0], p_sem.at[1])
    exchange(saved, core, 0).wait_send()
    for ref, number in weights:
        exchange(ref, core, number).wait_send()
    hand_over(hidden.at[1 - core], hidden_out, 4).wait_send()
    hand_over(deltas.at[1 - core], deltas_out, 5).wait_send()

    @pl.when(jnp.logical_not(is_last))
    def _():
        place_copy.wait_send()

    @pl.loop(0, steps)
    def _(d):
        spread_done(snd1.at[d], d1_send.at[d], d1_recv.at[d])
        rows_copy(core, d).wait_send()

        @pl.when(is_last)
        def _():
            spread_done(snd2.at[d], d2_send.at[d], d2_recv.at[1, d])

        @pl.when(jnp.logical_not(is_last))
        def _():
            piece(snd2.at[d], rcv2.at[0, d], below, d2_send.at[d], d2_recv.at[0, d]).wait_send()

        @pl.when(jnp.logical_not(is_first))
        def _():
            up_copy(d).wait_send()

    result.wait()
    for copy in (*kept, *saves(0), *saves(1)):
        copy.wait()


def weight_grads(
    units, near_ref, savedp_ref, rows_ref, deltas_ref, hidden_ref, out_ref, gg_ref, gu_ref, gd_ref
):
    count = savedp_ref.shape[0]
    tile = gd_ref.shape[2]
    here = pl.ds(pl.multiple_of(pl.program_id(0) * tile, 128), tile)
    out_ref[...] = near_ref[:, :, :, here]
    both = dot(savedp_ref[:, here], deltas_ref[...].reshape(count, 2 * units), 0, 0).astype(BF16)
    gg_ref[0] = both[:, :units]
    gu_ref[0] = both[:, units:]
    grad_rows = rows_ref[:, :, here].reshape(count, tile)
    gd_ref[0] = dot(hidden_ref[...].reshape(count, units), grad_rows, 0, 0).astype(BF16)


def body(expert_inputs, routes, gate_prob, out_grad, gate_weight, up_weight, down_weight):
    sections = lax.axis_size("pipe")
    members = lax.axis_size("expert")
    chips = members // 2
    tokens, features = out_grad.shape[1:]
    half = expert_inputs.shape[4]
    cap = 2 * half
    units = gate_weight.shape[2]
    side = chips * cap
    steps = 4
    lanes = features // steps // 128
    saved = expert_inputs[0, 0, 0].transpose(1, 0, 2).reshape(side, features)
    order = jnp.asarray(row_order(chips, half), BF16)
    vmem = pl.BlockSpec(memory_space=pltpu.VMEM)
    hbm = pl.BlockSpec(memory_space=pl.ANY)
    dma = pltpu.SemaphoreType.DMA
    moved = pltpu.VMEM((steps, side, lanes, 128), BF16)
    square = pltpu.VMEM((2, side, units), F32)
    near, savedp, rows, deltas, hidden = pl.pallas_call(
        functools.partial(relay, sections, chips, cap, steps),
        out_shape=(
            pltpu.VMEM((1, 1, tokens, features), BF16),
            pltpu.VMEM((2 * side, features), BF16),
            pltpu.VMEM((2, side, features), BF16),
            pltpu.VMEM((2, side, 2 * units), BF16),
            pltpu.VMEM((2, side, units), BF16),
        ),
        in_specs=[vmem] * 3 + [hbm] * 5,
        out_specs=(vmem,) * 5,
        scratch_shapes=[
            pltpu.VMEM((2, features, units), BF16),
            pltpu.VMEM((2, features, units), BF16),
            pltpu.VMEM((2, units, features), BF16),
            pltpu.VMEM((2, side, features), BF16),
            pltpu.VMEM((2 * side, features), BF16),
            pltpu.VMEM((2, side, features), BF16),
            moved,
            moved,
            moved,
            pltpu.VMEM((2, steps, side, lanes, 128), BF16),
            pltpu.VMEM((side, features), BF16),
            pltpu.VMEM((tokens, features), BF16),
            pltpu.VMEM((tokens, features), BF16),
            pltpu.VMEM((tokens, features), BF16),
            pltpu.VMEM((side, tokens), BF16),
            pltpu.VMEM((side, tokens), BF16),
            pltpu.VMEM((tokens, side), BF16),
            pltpu.VMEM((side, side), BF16),
            pltpu.VMEM((side, 1, 128), F32),
            pltpu.VMEM((side, 1, 128), F32),
            pltpu.VMEM((side, 128), F32),
            square,
            square,
            square,
            pltpu.VMEM((2, side, 2 * units), BF16),
            pltpu.VMEM((2, side, units), BF16),
            pltpu.VMEM((2, side, 2 * units), BF16),
            pltpu.VMEM((2, side, units), BF16),
            dma((5,)),
            dma((7,)),
        ]
        + [dma((steps,))] * 5
        + [dma((6,))] * 2
        + [dma((steps,))]
        + [dma((2, steps))]
        + [dma((steps,))] * 3
        + [dma((3,)), dma((2,))],
        compiler_params=pltpu.CompilerParams(
            collective_id=0, has_side_effects=True, vmem_limit_bytes=52 * 2**20
        ),
    )(
        routes.reshape(1, tokens),
        gate_prob.reshape(1, tokens),
        order,
        saved,
        out_grad,
        gate_weight,
        up_weight,
        down_weight,
    )
    tiles = 4
    tile = features // tiles
    return pl.pallas_call(
        functools.partial(weight_grads, units),
        grid=(tiles,),
        in_specs=[
            vmem,
            vmem,
            vmem,
            vmem,
            vmem,
        ],
        out_specs=(
            pl.BlockSpec((1, 1, tokens, tile), lambda i: (0, 0, 0, i)),
            pl.BlockSpec((1, tile, units), lambda i: (0, i, 0)),
            pl.BlockSpec((1, tile, units), lambda i: (0, i, 0)),
            pl.BlockSpec((1, units, tile), lambda i: (0, 0, i)),
        ),
        out_shape=(
            jax.ShapeDtypeStruct((1, 1, tokens, features), BF16),
            jax.ShapeDtypeStruct((1, features, units), BF16),
            jax.ShapeDtypeStruct((1, features, units), BF16),
            jax.ShapeDtypeStruct((1, units, features), BF16),
        ),
        compiler_params=pltpu.CompilerParams(vmem_limit_bytes=30 * 2**20),
    )(near, savedp, rows, deltas, hidden)


def solution(mesh):
    return jax.shard_map(
        body,
        mesh=mesh,
        in_specs=(
            P("pipe", None, "expert", None, None, None),
            P("pipe", None, "expert", None),
            P("pipe", None, "expert", None),
            P(None, "expert", None),
            P("pipe", None, "expert"),
            P("pipe", None, "expert"),
            P("pipe", "expert", None),
        ),
        out_specs=(
            P("pipe", None, "expert", None),
            P("pipe", None, "expert"),
            P("pipe", None, "expert"),
            P("pipe", "expert", None),
        ),
        check_vma=False,
    )
```

```python
import functools

import jax
import jax.numpy as jnp
import numpy as np
from jax import lax
from jax.experimental import pallas as pl
from jax.experimental.pallas import tpu as pltpu
from jax.sharding import PartitionSpec as P

MESH = pl.DeviceIdType.MESH
F32 = jnp.float32
BF16 = jnp.bfloat16


def dot(left, right, left_dim, right_dim):
    return lax.dot_general(
        left, right, (((left_dim,), (right_dim,)), ((), ())), preferred_element_type=F32
    )


def row_order(chips, half):
    cap = 2 * half
    side = chips * cap
    order = np.zeros((2 * side, 2 * side), np.float32)
    for core in range(2):
        for chip in range(chips):
            for c in range(cap):
                source = (c // half) * side + (c % half) * 2 * chips + 2 * chip + core
                order[core * side + chip * cap + c, source] = 1.0
    return order


def relay(
    sections,
    chips,
    cap,
    steps,
    route_ref,
    prob_ref,
    order_ref,
    saved_hbm,
    grad_hbm,
    wg_hbm,
    wu_hbm,
    wd_hbm,
    out_kept,
    savedp_kept,
    rows_kept,
    deltas_kept,
    hidden_kept,
    wg,
    wu,
    wd,
    saved,
    savedp,
    rows,
    snd1,
    rcv1,
    snd2,
    rcv2,
    raw,
    up,
    res,
    fin,
    place,
    place_up,
    place_t,
    mix,
    psnd,
    prcv,
    prob_of,
    pre_g,
    pre_u,
    dh,
    deltas,
    hidden,
    deltas_out,
    hidden_out,
    in_sem,
    out_sem,
    d1_send,
    d1_recv,
    d1_own,
    rx_send,
    rx_recv,
    x_send,
    x_recv,
    d2_send,
    d2_recv,
    d2_own,
    z_send,
    z_recv,
    p_sem,
    q_sem,
):
    section = lax.axis_index("pipe")
    me = lax.axis_index("expert")
    chip = me // 2
    core = me % 2
    side = chips * cap
    features = up.shape[1]
    units = wg.shape[2]
    width = features // steps
    lanes = width // 128
    partner = (section, 2 * chip + 1 - core)
    is_first = section == sections - 1
    is_last = section == 0
    below = (lax.rem(section + sections - 1, sections), me)
    above = (lax.rem(section + 1, sections), me)
    far = side - cap

    def cols(d):
        return pl.ds(pl.multiple_of(d * width, 128), width)

    depth = min(4, chips)
    height = chips // depth
    offsets = sorted(
        ((i, j) for i in range(height) for j in range(depth)),
        key=lambda o: -min(o[0], height - o[0]) - min(o[1], depth - o[1]),
    )
    others = [
        lax.rem(chip // depth + i, height) * depth + lax.rem(chip % depth + j, depth)
        for i, j in offsets
    ]

    barrier = pltpu.get_barrier_semaphore()

    def greet(target):
        pl.semaphore_signal(barrier, inc=1, device_id=target, device_id_type=MESH)

    greet(partner)

    for other in others[:-1]:
        greet((section, 2 * other + core))

    @pl.when(jnp.logical_not(is_first))
    def _():
        for other in others:
            greet((above[0], 2 * other + core))

    @pl.when(jnp.logical_not(is_last))
    def _():
        for other in others:
            greet((below[0], 2 * other + core))

    loads = [
        pltpu.make_async_copy(saved_hbm, saved.at[core], in_sem.at[0]),
        pltpu.make_async_copy(wg_hbm.at[0], wg.at[core], in_sem.at[1]),
        pltpu.make_async_copy(wu_hbm.at[0], wu.at[core], in_sem.at[2]),
        pltpu.make_async_copy(wd_hbm.at[0], wd.at[core], in_sem.at[3]),
    ]
    first = pltpu.make_async_copy(grad_hbm.at[0], up, in_sem.at[4])

    @pl.when(is_first)
    def _():
        first.start()

    for load in loads:
        load.start()

    tokens = route_ref.shape[1]
    experts = lax.broadcasted_iota(jnp.int32, (max(chips, 8), tokens), 0)
    member = (route_ref[...] == experts).astype(F32)
    earlier = (
        lax.broadcasted_iota(jnp.int32, (tokens, tokens), 0)
        < lax.broadcasted_iota(jnp.int32, (tokens, tokens), 1)
    )
    before = dot(member.astype(BF16), earlier.astype(BF16), 1, 0)
    rank = jnp.sum(before * member, axis=0, keepdims=True)
    slot = route_ref[...].astype(F32) * cap + rank
    slots = lax.broadcasted_iota(jnp.int32, (side, tokens), 0).astype(F32)
    to_slot = (slot == slots).astype(F32)
    place[...] = to_slot.astype(BF16)
    prob_slot = jnp.sum(to_slot * prob_ref[...], axis=1, keepdims=True)
    psnd[...] = jnp.broadcast_to(prob_slot, (side, 128)).reshape(side, 1, 128)

    pl.semaphore_wait(barrier, jnp.where(is_first | is_last, 2 * chips, 3 * chips))

    def piece(src, dst, target, send_sem, recv_sem):
        return pltpu.make_async_remote_copy(
            src_ref=src,
            dst_ref=dst,
            send_sem=send_sem,
            recv_sem=recv_sem,
            device_id=target,
            device_id_type=MESH,
        )

    mine = pl.ds(chip * cap, cap)
    most = pl.ds(0, far)

    def spread(src, dst, send, recv, keep):
        pltpu.make_async_copy(src.at[mine], dst.at[mine], keep).start()

        for other in others[:-1]:
            target = (section, 2 * other + core)
            piece(src.at[pl.ds(other * cap, cap)], dst.at[mine], target, send, recv).start()

    def collect(src, dst, send, recv, keep):
        pltpu.make_async_copy(src.at[mine], dst.at[mine], keep).wait()
        piece(src.at[most], dst.at[most], partner, send, recv).wait_recv()

    def spread_done(src, send, recv):
        piece(src.at[most], src.at[most], partner, send, recv).wait_send()

    def to_partner(src, dst, send_sem, recv_sem):
        return piece(src, dst, partner, send_sem, recv_sem)

    def rows_copy(p, d):
        here = rows.at[p, :, cols(d)]
        return to_partner(here, here, rx_send.at[d], rx_recv.at[d])

    def exchange(ref, at, number):
        return to_partner(ref.at[at], ref.at[at], x_send.at[number], x_recv.at[number])

    weights = ((wd, 3), (wg, 1), (wu, 2))

    def hand_over(src, dst, number):
        return to_partner(src, dst.at[core], x_send.at[number], x_recv.at[number])

    def arrival(dst, number):
        return to_partner(dst.at[1 - core], dst.at[1 - core], x_send.at[number], x_recv.at[number])

    place_copy = piece(place, place_up, below, q_sem.at[0], q_sem.at[1])

    def up_copy(d):
        return piece(res.at[:, cols(d)], fin.at[:, cols(d)], above, z_send.at[d], z_recv.at[d])

    def dispatch(d):
        @pl.when(is_first)
        def _():
            placed = dot(place[...], up[:, cols(d)], 1, 0).astype(BF16)
            snd1[d] = placed.reshape(side, lanes, 128)

        @pl.when(jnp.logical_not(is_first))
        def _():
            piece(snd2.at[d], rcv2.at[0, d], above, d2_send.at[d], d2_recv.at[0, d]).wait_recv()
            moved = dot(mix[...], rcv2[0, d].reshape(side, width), 1, 0).astype(BF16)
            snd1[d] = moved.reshape(side, lanes, 128)

        spread(snd1.at[d], rcv1.at[d], d1_send.at[d], d1_recv.at[d], d1_own.at[d])

    def assemble(d):
        res[:, cols(d)] = dot(place_t[...], rcv2[0, d].reshape(side, width), 1, 0).astype(BF16)
        up_copy(d).start()

    def take(d):
        collect(snd1.at[d], rcv1.at[d], d1_send.at[d], d1_recv.at[d], d1_own.at[d])
        now = rcv1[d].reshape(side, width)
        raw[:, cols(d)] = now
        scaled = (prob_of[:, :1] * now.astype(F32)).astype(BF16)
        rows[core, :, cols(d)] = scaled
        for half in range(2):
            dh[half] += dot(scaled, wd[half, :, cols(d)], 1, 1)
        rows_copy(core, d).start()

    def pre(half):
        @pl.loop(0, steps)
        def _(d):
            now = savedp[pl.ds(pl.multiple_of(core * side, 16), side), cols(d)]
            pre_g[half] += dot(now, wg[half, cols(d), :], 1, 0)
            pre_u[half] += dot(now, wu[half, cols(d), :], 1, 0)

        gate = pre_g[half]
        pre_up = pre_u[half]
        sigmoid = jax.nn.sigmoid(gate)
        silu = gate * sigmoid
        hidden[half] = (silu * pre_up).astype(BF16)
        pre_u[half] = silu
        pre_g[half] = pre_up * sigmoid * (1.0 + gate * (1.0 - sigmoid))

    def forward():
        exchange(saved, 1 - core, 0).wait_recv()
        pre_g[...] = jnp.zeros_like(pre_g)
        pre_u[...] = jnp.zeros_like(pre_u)

        @pl.loop(0, steps)
        def _(d):
            mixed = saved[:, :, cols(d)].reshape(2 * side, width)
            savedp[:, cols(d)] = dot(order_ref[...], mixed, 1, 0).astype(BF16)

        pre(core)
        exchange(wd, 1 - core, 3).wait_recv()

    def forward_rest():
        for ref, number in weights[1:]:
            exchange(ref, 1 - core, number).wait_recv()
        pre(1 - core)
        hidden_out[core] = hidden[core]
        hand_over(hidden.at[1 - core], hidden_out, 4).start()

    def make_deltas():
        for half in range(2):
            delta = dh[half]
            deltas[half, :, :units] = (delta * pre_g[half]).astype(BF16)
            deltas[half, :, units:] = (delta * pre_u[half]).astype(BF16)
        deltas_out[core] = deltas[core]
        hand_over(deltas.at[1 - core], deltas_out, 5).start()

    def saves(p):
        return (
            pltpu.make_async_copy(rows.at[p], rows_kept.at[p], out_sem.at[3 + 2 * p]),
            pltpu.make_async_copy(deltas_out.at[p], deltas_kept.at[p], out_sem.at[4 + 2 * p]),
        )

    def part(half, d):
        here = cols(d)
        both = dot(deltas[half, :, :units], wg[half, here, :], 1, 1)
        both += dot(deltas[half, :, units:], wu[half, here, :], 1, 1)
        return both.astype(BF16).astype(F32)

    def give(d):
        back = (part(0, d) + part(1, d)).astype(BF16)
        total = raw[:, cols(d)].astype(F32) + back.astype(F32)
        snd2[d] = total.astype(BF16).reshape(side, lanes, 128)

        @pl.when(jnp.logical_not(is_last))
        def _():
            for other in others:
                piece(
                    snd2.at[d, pl.ds(other * cap, cap)],
                    rcv2.at[0, d, mine],
                    (below[0], 2 * other + core),
                    d2_send.at[d],
                    d2_recv.at[0, d],
                ).start()

        @pl.when(is_last)
        def _():
            spread(snd2.at[d], rcv2.at[1, d], d2_send.at[d], d2_recv.at[1, d], d2_own.at[d])

    def finish(d):
        collect(snd2.at[d], rcv2.at[1, d], d2_send.at[d], d2_recv.at[1, d], d2_own.at[d])
        fin[:, cols(d)] = dot(place[...], rcv2[1, d].reshape(side, width), 0, 0).astype(BF16)

    @pl.when(is_first)
    def _():
        first.wait()

        @pl.when(core == 0)
        def _():
            pl.loop(0, steps)(dispatch)

    @pl.when(jnp.logical_not(is_last))
    def _():
        place_copy.start()

    spread(psnd, prcv, p_sem.at[0], p_sem.at[1], p_sem.at[2])

    loads[0].wait()
    exchange(saved, core, 0).start()
    for ref, number in weights:
        loads[number].wait()
        exchange(ref, core, number).start()

    forward()
    collect(psnd, prcv, p_sem.at[0], p_sem.at[1], p_sem.at[2])
    prob_of[...] = prcv[...].reshape(side, 128)

    @pl.when(jnp.logical_not(is_first))
    def _():
        forward_rest()
        place_copy.wait_recv()
        mix[...] = dot(place[...], place_up[...], 1, 1).astype(BF16)
        place_t[...] = place_up[...].astype(F32).T.astype(BF16)

    kept = (
        pltpu.make_async_copy(savedp, savedp_kept, out_sem.at[1]),
        pltpu.make_async_copy(hidden_out, hidden_kept, out_sem.at[2]),
    )
    kept[0].start()
    result = pltpu.make_async_copy(fin, out_kept.at[0, 0], out_sem.at[0])
    dh[...] = jnp.zeros_like(dh)

    def partners_share():
        @pl.when(jnp.logical_not(is_first & (core == 1)))
        def _():
            pl.loop(0, steps)(lambda d: rows_copy(1 - core, d).wait_recv())

        arrival(hidden_out, 4).wait_recv()
        arrival(deltas_out, 5).wait_recv()
        kept[1].start()
        for copy in saves(1 - core):
            copy.start()

    @pl.when(is_first & (core == 1))
    def _():
        pl.loop(0, steps)(lambda d: rows_copy(0, d).wait_recv())

    @pl.loop(0, steps + 3)
    def _(d):
        @pl.when((d < steps) & jnp.logical_not(is_first & (core == 0)))
        def _():
            dispatch(d)

        @pl.when((d < steps) & jnp.logical_not(is_first))
        def _():
            assemble(d)

        @pl.when(d >= 3)
        def _():
            take(d - 3)

    @pl.when(is_first)
    def _():
        forward_rest()

    make_deltas()
    pl.loop(0, steps)(give)
    for copy in saves(core):
        copy.start()

    @pl.when(core == 1)
    def _():
        partners_share()

    @pl.when(is_last)
    def _():
        pl.loop(0, steps)(finish)

    @pl.when(jnp.logical_not(is_last))
    def _():
        @pl.loop(0, steps)
        def _(d):
            up_copy(d).wait_recv()

    result.start()

    @pl.when(core == 0)
    def _():
        partners_share()

    spread_done(psnd, p_sem.at[0], p_sem.at[1])
    exchange(saved, core, 0).wait_send()
    for ref, number in weights:
        exchange(ref, core, number).wait_send()
    hand_over(hidden.at[1 - core], hidden_out, 4).wait_send()
    hand_over(deltas.at[1 - core], deltas_out, 5).wait_send()

    @pl.when(jnp.logical_not(is_last))
    def _():
        place_copy.wait_send()

    @pl.loop(0, steps)
    def _(d):
        spread_done(snd1.at[d], d1_send.at[d], d1_recv.at[d])
        rows_copy(core, d).wait_send()

        @pl.when(is_last)
        def _():
            spread_done(snd2.at[d], d2_send.at[d], d2_recv.at[1, d])

        @pl.when(jnp.logical_not(is_last))
        def _():
            piece(snd2.at[d], rcv2.at[0, d], below, d2_send.at[d], d2_recv.at[0, d]).wait_send()

        @pl.when(jnp.logical_not(is_first))
        def _():
            up_copy(d).wait_send()

    result.wait()
    for copy in (*kept, *saves(0), *saves(1)):
        copy.wait()


def weight_grads(
    units, near_ref, savedp_ref, rows_ref, deltas_ref, hidden_ref, out_ref, gg_ref, gu_ref, gd_ref
):
    count = savedp_ref.shape[0]
    tile = gd_ref.shape[2]
    here = pl.ds(pl.multiple_of(pl.program_id(0) * tile, 128), tile)
    out_ref[...] = near_ref[:, :, :, here]
    both = dot(savedp_ref[:, here], deltas_ref[...].reshape(count, 2 * units), 0, 0).astype(BF16)
    gg_ref[0] = both[:, :units]
    gu_ref[0] = both[:, units:]
    grad_rows = rows_ref[:, :, here].reshape(count, tile)
    gd_ref[0] = dot(hidden_ref[...].reshape(count, units), grad_rows, 0, 0).astype(BF16)


def body(expert_inputs, routes, gate_prob, out_grad, gate_weight, up_weight, down_weight):
    sections = lax.axis_size("pipe")
    members = lax.axis_size("expert")
    chips = members // 2
    tokens, features = out_grad.shape[1:]
    half = expert_inputs.shape[4]
    cap = 2 * half
    units = gate_weight.shape[2]
    side = chips * cap
    steps = 4
    lanes = features // steps // 128
    saved = expert_inputs[0, 0, 0].transpose(1, 0, 2).reshape(side, features)
    order = jnp.asarray(row_order(chips, half), BF16)
    vmem = pl.BlockSpec(memory_space=pltpu.VMEM)
    hbm = pl.BlockSpec(memory_space=pl.ANY)
    dma = pltpu.SemaphoreType.DMA
    moved = pltpu.VMEM((steps, side, lanes, 128), BF16)
    square = pltpu.VMEM((2, side, units), F32)
    near, savedp, rows, deltas, hidden = pl.pallas_call(
        functools.partial(relay, sections, chips, cap, steps),
        out_shape=(
            pltpu.VMEM((1, 1, tokens, features), BF16),
            pltpu.VMEM((2 * side, features), BF16),
            pltpu.VMEM((2, side, features), BF16),
            pltpu.VMEM((2, side, 2 * units), BF16),
            pltpu.VMEM((2, side, units), BF16),
        ),
        in_specs=[vmem] * 3 + [hbm] * 5,
        out_specs=(vmem,) * 5,
        scratch_shapes=[
            pltpu.VMEM((2, features, units), BF16),
            pltpu.VMEM((2, features, units), BF16),
            pltpu.VMEM((2, units, features), BF16),
            pltpu.VMEM((2, side, features), BF16),
            pltpu.VMEM((2 * side, features), BF16),
            pltpu.VMEM((2, side, features), BF16),
            moved,
            moved,
            moved,
            pltpu.VMEM((2, steps, side, lanes, 128), BF16),
            pltpu.VMEM((side, features), BF16),
            pltpu.VMEM((tokens, features), BF16),
            pltpu.VMEM((tokens, features), BF16),
            pltpu.VMEM((tokens, features), BF16),
            pltpu.VMEM((side, tokens), BF16),
            pltpu.VMEM((side, tokens), BF16),
            pltpu.VMEM((tokens, side), BF16),
            pltpu.VMEM((side, side), BF16),
            pltpu.VMEM((side, 1, 128), F32),
            pltpu.VMEM((side, 1, 128), F32),
            pltpu.VMEM((side, 128), F32),
            square,
            square,
            square,
            pltpu.VMEM((2, side, 2 * units), BF16),
            pltpu.VMEM((2, side, units), BF16),
            pltpu.VMEM((2, side, 2 * units), BF16),
            pltpu.VMEM((2, side, units), BF16),
            dma((5,)),
            dma((7,)),
        ]
        + [dma((steps,))] * 5
        + [dma((6,))] * 2
        + [dma((steps,))]
        + [dma((2, steps))]
        + [dma((steps,))] * 3
        + [dma((3,)), dma((2,))],
        compiler_params=pltpu.CompilerParams(
            collective_id=0, has_side_effects=True, vmem_limit_bytes=52 * 2**20
        ),
    )(
        routes.reshape(1, tokens),
        gate_prob.reshape(1, tokens),
        order,
        saved,
        out_grad,
        gate_weight,
        up_weight,
        down_weight,
    )
    tiles = 4
    tile = features // tiles
    return pl.pallas_call(
        functools.partial(weight_grads, units),
        grid=(tiles,),
        in_specs=[
            vmem,
            vmem,
            vmem,
            vmem,
            vmem,
        ],
        out_specs=(
            pl.BlockSpec((1, 1, tokens, tile), lambda i: (0, 0, 0, i)),
            pl.BlockSpec((1, tile, units), lambda i: (0, i, 0)),
            pl.BlockSpec((1, tile, units), lambda i: (0, i, 0)),
            pl.BlockSpec((1, units, tile), lambda i: (0, 0, i)),
        ),
        out_shape=(
            jax.ShapeDtypeStruct((1, 1, tokens, features), BF16),
            jax.ShapeDtypeStruct((1, features, units), BF16),
            jax.ShapeDtypeStruct((1, features, units), BF16),
            jax.ShapeDtypeStruct((1, units, features), BF16),
        ),
        compiler_params=pltpu.CompilerParams(vmem_limit_bytes=30 * 2**20),
    )(near, savedp, rows, deltas, hidden)


def solution(mesh):
    return jax.shard_map(
        body,
        mesh=mesh,
        in_specs=(
            P("pipe", None, "expert", None, None, None),
            P("pipe", None, "expert", None),
            P("pipe", None, "expert", None),
            P(None, "expert", None),
            P("pipe", None, "expert"),
            P("pipe", None, "expert"),
            P("pipe", "expert", None),
        ),
        out_specs=(
            P("pipe", None, "expert", None),
            P("pipe", None, "expert"),
            P("pipe", None, "expert"),
            P("pipe", "expert", None),
        ),
        check_vma=False,
    )
```
